128 devices in a mesh: tile: 32 (over y, x, core), band: 4 (over z).
Axes of the slice: x: 4, y: 4, z: 4, core: 2. Of those that a mesh axis runs over, the one named last changes fastest.
Arguments:
- noisy: bfloat16 [12, 1024, 512], P(None, 'tile', 'band'), may hold values from -6 to 6
- grad_pred: bfloat16 [12, 1024, 512], P(None, 'tile', 'band'), may hold values from -6 to 6
- coarse: bfloat16 [4, 64, 38, 128], P('band'), may hold values from -6 to 6
- margin_band: int32 [1024, 1], P(('tile', 'band')), may hold values from 0 to 3; in each aligned block of 8 rows (0 to 7, 8 to 15, ...) at most 4 rows name the same one
- margin_slot: int32 [1024], P(('tile', 'band')), may hold values from 0 to 63
- interp: bfloat16 [32, 4, 8, 128, 4096], P('tile', 'band'), may hold values from -0.1875 to 0.1875
- w_in: bfloat16 [128, 50], replicated, may hold values from -0.875 to 0.875
- w_conv1: bfloat16 [3, 3, 128, 128], replicated, may hold values from -0.1875 to 0.1875
- w_conv2: bfloat16 [3, 3, 128, 128], replicated, may hold values from -0.1875 to 0.1875
- w_out: bfloat16 [12, 128], replicated, may hold values from -0.5 to 0.5
Outputs:
- pred: float32 [12, 1024, 512], P(None, 'tile', 'band')
- coarse_grad: float32 [4, 64, 38, 128], P('band', 'tile')
- grad_in: float32 [128, 50], replicated
- grad_conv1: float32 [3, 3, 128, 128], replicated
- grad_conv2: float32 [3, 3, 128, 128], replicated
- grad_out: float32 [12, 128], replicated
The draws below stay inside these ranges and needn't reach their ends.
Inputs may be any that keep to these rules, and one draw needn't show every extreme that they name: `margin_band`: of the 8 entries of one device, at most 4 name the same band, and every draw has devices where one band is named exactly 4 times.
All inputs are finite; a program needn't handle non-finite values.
Results may differ from the reference program's by a relative error of at most 0.015.
Values may be sent and summed in bfloat16 or wider, within the bound.
No kernel may reach another device: no remote copies, remote signals or barrier semaphores. Data moves between devices by JAX's collectives and lax.ppermute only.
A program may use at most 128 MiB of HBM per device.

```python
import math
import jax
import jax.numpy as jnp
import numpy as np
from jax import lax

CH = 128
CO = 12
CC = 38
TH = 32
TW = 128
CBC = 128
CB_BAND = 64
K = 8
MOST = 4
NH = 1024
NW = 512
N_TILE = 32
N_BAND = 4


def touch_ends(array, stream_key, smallest, high):
    longest = array.shape.index(max(array.shape))
    spots = []
    for shift in (0, 1):
        where = [jax.random.randint(jax.random.fold_in(stream_key, axis), (), 0, length) for axis, length in enumerate(array.shape)]
        where[longest] = (where[longest] + shift) % array.shape[longest]
        spots.append(tuple(where))
    return array.at[spots[0]].set(smallest).at[spots[1]].set(high)


def block_levels(key, dims, pieces, low, largest):
    gain = 1.0
    for axis_at, blocks in pieces:
        heights = jax.random.uniform(jax.random.fold_in(jax.random.fold_in(key, 6), axis_at), (blocks,), jnp.float32, low / len(pieces), largest / len(pieces))
        gain = gain * jnp.repeat(jnp.exp(heights), dims[axis_at] // blocks).reshape((-1,) + (1,) * (len(dims) - 1 - axis_at))
    return gain


def deal_out(key, own, number, rows, count, top, reach, slope):
    ranking = jax.random.permutation(key, count)
    heavy_load, common = portions_of(count, rows * top, reach, slope, True), portions_of(count, rows * top, reach, slope, False)
    places = jnp.arange(count)

    def named(sizes, turn):
        used = int((sizes > 0).sum())
        fixed = max(1, used // 4)
        moved = fixed + (places - fixed + turn * (used - fixed)) % max(1, count - fixed)
        return jnp.zeros((count,), jnp.int32).at[ranking[jnp.where(places < fixed, places, moved)]].set(jnp.asarray(sizes, jnp.int32))

    sizes = jnp.where(number % 4 == 0, named(heavy_load, number // 4), named(common, number - number // 4 - 1))
    mixed = jax.random.permutation(jax.random.fold_in(own, 3), count)
    source_of, taker = mixed[0:count // 2 * 2:2], mixed[1:count // 2 * 2:2]
    slack = jnp.minimum(sizes[source_of] - 1, reach - sizes[taker]) // 2
    slack = jnp.where((source_of == ranking[0]) | (taker == ranking[0]) | (sizes[taker] == 0), 0, jnp.maximum(slack, 0))
    moved = jax.random.randint(jax.random.fold_in(own, 4), (count // 2,), 0, 1 << 20) % (slack + 1)
    sizes = sizes.at[source_of].add(-moved).at[taker].add(moved)
    items = jnp.searchsorted(jnp.cumsum(sizes), jnp.arange(rows * top), side="right").astype(jnp.int32)
    listing = items.reshape(top, rows).T
    listing = listing[jax.random.permutation(jax.random.fold_in(own, 1), rows)]
    turn = jax.random.randint(jax.random.fold_in(own, 2), (rows, 1), 0, top)
    return jnp.take_along_axis(listing, (jnp.arange(top)[None, :] + turn) % top, axis=1)


def portions_of(number_of, total, most, slope, full):
    loads = [(1 << 20) // math.isqrt(rank ** slope) + 1 for rank in range(1, number_of + 1)]
    largest = most if full else min(most, max(-(-total // number_of), total * loads[0] // sum(loads)))
    least = 1 if total - largest >= number_of - 1 else 0
    counts, spare = [largest] + [least] * (number_of - 1), total - largest - least * (number_of - 1)
    while spare > 0:
        candidates = [i for i in range(1, number_of) if counts[i] < largest] or [i for i in range(1, number_of) if counts[i] < most]
        whole, remaining = sum([loads[i] for i in candidates]), spare
        for i in candidates:
            more = min(most - counts[i], max(1, remaining * loads[i] // whole), spare)
            counts[i] = counts[i] + more
            spare = spare - more
    return np.array(counts)


def bell_draw(stream_key, extent, width, most, split=(), dtype=jnp.bfloat16):
    factor_of = block_levels(stream_key, extent, split, -0.22, 0.18) if split else 1.0
    entries = jax.random.normal(stream_key, extent, jnp.float32) * width * factor_of
    return jnp.minimum(jnp.maximum(entries, -most), most).astype(dtype)


def setup_inputs(seed: int = 0) -> dict:
    arg_keys = jax.random.split(jax.random.key(seed), 11)
    noisy = bell_draw(arg_keys[0], (CO, NH, NW), 1.0, 6.0, ((1, 32), (2, 4)))
    grad_pred = bell_draw(arg_keys[1], (CO, NH, NW), 1.0, 6.0, ((1, 32), (2, 4)))
    coarse = bell_draw(arg_keys[2], (N_BAND, CB_BAND, CC, CBC), 1.0, 6.0, ((0, 4),))
    margin_band_keys = jax.random.split(jax.random.fold_in(arg_keys[3], 1), (N_TILE * N_BAND * K) // K)
    margin_band_turns = jax.random.permutation(jax.random.fold_in(arg_keys[3], 3), (N_TILE * N_BAND * K) // K)
    margin_band = jax.vmap(lambda own, number: deal_out(jax.random.fold_in(arg_keys[3], 2), own, number, K, N_BAND, 1, MOST, 2))(margin_band_keys, margin_band_turns).reshape((N_TILE * N_BAND * K, 1))
    margin_slot = touch_ends(jax.random.randint(arg_keys[4], (N_TILE * N_BAND * K,), 0, CB_BAND), jax.random.fold_in(arg_keys[4], 1), 0, CB_BAND - 1).astype(jnp.int32)
    interp = bell_draw(arg_keys[5], (N_TILE, N_BAND, K, CBC, TH * TW), (K * CBC) ** -0.5, 0.1875, ((0, 32), (1, 4)))
    w_in = bell_draw(arg_keys[6], (CH, CC + CO), (CC + CO) ** -0.5, 0.875)
    w_conv1 = bell_draw(arg_keys[7], (3, 3, CH, CH), (9 * CH) ** -0.5, 0.1875)
    w_conv2 = bell_draw(arg_keys[8], (3, 3, CH, CH), (9 * CH) ** -0.5, 0.1875)
    w_out = bell_draw(arg_keys[9], (CO, CH), CH ** -0.5, 0.5)
    return {"noisy": noisy, "grad_pred": grad_pred, "coarse": coarse, "margin_band": margin_band, "margin_slot": margin_slot, "interp": interp, "w_in": w_in, "w_conv1": w_conv1, "w_conv2": w_conv2, "w_out": w_out}


def multiply(left, right):
    return jnp.dot(left.astype(jnp.float32), right.astype(jnp.float32), precision=lax.Precision.HIGHEST)

def multiply_nt(left, right):
    return jnp.dot(left.astype(jnp.float32), right.astype(jnp.float32).T, precision=lax.Precision.HIGHEST)

def silu_slope(value):
    sig = jax.nn.sigmoid(value)
    return sig * (1.0 + value * (1.0 - sig))

def shifted(field, rows, cols, p_tap, q_tap, flip):
    chans = field.shape[0]
    padded = jnp.pad(field.reshape(chans, rows, cols), ((0, 0), (1, 1), (1, 1)))
    r_start = 2 - p_tap if flip else p_tap
    c_start = 2 - q_tap if flip else q_tap
    return padded[:, r_start:r_start + rows, c_start:c_start + cols].reshape(chans, rows * cols)

def conv_fwd(field, weight, rows, cols):
    total = jnp.zeros((weight.shape[2], rows * cols), jnp.float32)
    for p_tap in range(3):
        for q_tap in range(3):
            total = total + multiply(weight[p_tap, q_tap], shifted(field, rows, cols, p_tap, q_tap, False))
    return total

def conv_bwd(grad, weight, rows, cols):
    total = jnp.zeros((weight.shape[3], rows * cols), jnp.float32)
    for p_tap in range(3):
        for q_tap in range(3):
            total = total + multiply(weight[p_tap, q_tap].T, shifted(grad, rows, cols, p_tap, q_tap, True))
    return total

def conv_wgrad(grad, field, rows, cols):
    taps = []
    for p_tap in range(3):
        for q_tap in range(3):
            taps.append(multiply_nt(grad, shifted(field, rows, cols, p_tap, q_tap, False)))
    return jnp.stack(taps, 0).reshape(3, 3, grad.shape[0], field.shape[0])

def reference(noisy, grad_pred, coarse, margin_band, margin_slot, interp, w_in, w_conv1, w_conv2, w_out):
    rows = TH * N_TILE
    cols = TW * N_BAND
    n_all = rows * cols
    cells = TH * TW
    block_ids = (margin_band[:, 0].astype(jnp.int32) * CB_BAND + margin_slot.astype(jnp.int32)).astype(jnp.int32)
    flat_coarse = coarse.reshape(N_BAND * CB_BAND, CC, CBC)
    picked = flat_coarse[block_ids].reshape(N_TILE, N_BAND, K, CC, CBC)

    def interp_tile(pair):
        blocks, weights = pair
        return jnp.einsum('bkcm,bkmn->bcn', blocks.astype(jnp.float32), weights.astype(jnp.float32), precision=lax.Precision.HIGHEST)
    cond_dev = lax.map(interp_tile, (picked, interp))
    cond = cond_dev.astype(jnp.bfloat16).reshape(N_TILE, N_BAND, CC, TH, TW).transpose(2, 0, 3, 1, 4).reshape(CC, n_all)
    inputs = jnp.concatenate([cond, noisy.reshape(CO, n_all)], 0)
    h_zero = multiply(w_in, inputs)
    a_zero = jax.nn.silu(h_zero).astype(jnp.bfloat16)
    z_one = conv_fwd(a_zero, w_conv1, rows, cols)
    a_one = jax.nn.silu(z_one).astype(jnp.bfloat16)
    z_two = conv_fwd(a_one, w_conv2, rows, cols)
    a_two = (a_zero.astype(jnp.float32) + z_two).astype(jnp.bfloat16)
    pred = multiply(w_out, a_two)
    cotangent = grad_pred.reshape(CO, n_all)
    d_two = multiply(w_out.T, cotangent).astype(jnp.bfloat16)
    d_one = (conv_bwd(d_two, w_conv2, rows, cols) * silu_slope(z_one)).astype(jnp.bfloat16)
    d_zero = ((conv_bwd(d_one, w_conv1, rows, cols) + d_two.astype(jnp.float32)) * silu_slope(h_zero)).astype(jnp.bfloat16)
    d_cond = multiply(w_in[:, :CC].T, d_zero).astype(jnp.bfloat16)
    d_dev = d_cond.reshape(CC, N_TILE, TH, N_BAND, TW).transpose(1, 3, 0, 2, 4).reshape(N_TILE, N_BAND, CC, cells)

    def back_tile(pair):
        grads, weights = pair
        return jnp.einsum('bcn,bkmn->bkcm', grads.astype(jnp.float32), weights.astype(jnp.float32), precision=lax.Precision.HIGHEST)
    d_blocks = lax.map(back_tile, (d_dev, interp))
    coarse_grad = jax.ops.segment_sum(d_blocks.reshape(N_TILE * N_BAND * K, CC, CBC), block_ids, num_segments=N_BAND * CB_BAND)
    coarse_grad = coarse_grad.reshape(N_BAND, CB_BAND, CC, CBC)
    factor = 1.0 / math.sqrt(n_all)
    grad_in = multiply_nt(d_zero, inputs) * factor
    grad_conv1 = conv_wgrad(d_one, a_zero, rows, cols) * factor
    grad_conv2 = conv_wgrad(d_two, a_one, rows, cols) * factor
    grad_out = multiply_nt(cotangent, a_two) * factor
    return (pred.reshape(CO, rows, cols), coarse_grad, grad_in, grad_conv1, grad_conv2, grad_out)
```

```python
import functools
import math

import jax
import jax.numpy as jnp
import numpy as np
from jax import lax
from jax.experimental import pallas as pl
from jax.experimental.pallas import tpu as pltpu
from jax.sharding import PartitionSpec as P

MOST = 4
ALL = ("tile", "band")

PITCH = 132
HIGH = 36
SPAN = 4864
GUARD = 256
STEP = 256
STEPS = SPAN // STEP
FEED = 80
NOISY_AT = 48
GRAD_AT = 60
CHUNK = 24
NT = (((1,), (1,)), ((), ()))


def f32dot(left, right):
    return jnp.dot(left, right, preferred_element_type=jnp.float32)


def vmem(limit=56 * 1024 * 1024):
    return pltpu.CompilerParams(vmem_limit_bytes=limit)


def whole():
    return pl.BlockSpec(memory_space=pltpu.VMEM)


def scalars():
    return pl.BlockSpec(memory_space=pltpu.SMEM)


def plan_kernel(band_ref, slot_ref, place_ref, wanted_ref):
    count = slot_ref.shape[0]
    for i in range(wanted_ref.shape[0]):
        wanted_ref[i] = jnp.int32(-1)
    for j in range(count):
        band = band_ref[j]
        rank = jnp.int32(0)
        for i in range(j):
            rank = rank + jnp.where(band_ref[i] == band, 1, 0)
        place = band * MOST + rank
        place_ref[j] = place
        wanted_ref[place] = slot_ref[j]


def plan(bands, slots, total):
    return pl.pallas_call(
        plan_kernel,
        out_shape=(
            jax.ShapeDtypeStruct(slots.shape, jnp.int32),
            jax.ShapeDtypeStruct((total,), jnp.int32),
        ),
        in_specs=[scalars(), scalars()],
        out_specs=(scalars(), scalars()),
    )(bands, slots)


def serve_kernel(asked_ref, coarse_ref, out_ref):
    for i in range(out_ref.shape[0]):
        out_ref[i] = coarse_ref[jnp.maximum(asked_ref[i], 0)]


def serve(asked, coarse):
    return pl.pallas_call(
        serve_kernel,
        out_shape=jax.ShapeDtypeStruct((asked.shape[0],) + coarse.shape[1:], coarse.dtype),
        in_specs=[scalars(), whole()],
        out_specs=whole(),
        compiler_params=vmem(),
    )(asked, coarse)


def feed_kernel(place_ref, arrived_ref, interp_ref, given_ref, feed_ref, edge_ref, picked):
    step = pl.program_id(0)
    ch = arrived_ref.shape[1]
    count = interp_ref.shape[0]
    cells = interp_ref.shape[1]
    lanes = interp_ref.shape[2]

    @pl.when(step == 0)
    def _():
        edge_ref[...] = jnp.zeros_like(edge_ref)
        for j in range(count):
            picked[:, j * cells : (j + 1) * cells] = arrived_ref[place_ref[j]]

    matrix = interp_ref[...].reshape(count * cells, lanes)
    cond = f32dot(picked[...], matrix).astype(jnp.bfloat16)
    feed_ref[...] = jnp.zeros_like(feed_ref)
    feed_ref[0:ch, :] = cond
    feed_ref[NOISY_AT:, :] = given_ref[...]
    rows = lanes // 128
    at = lax.broadcasted_iota(jnp.int32, (lanes, 128), 0)
    lane = lax.broadcasted_iota(jnp.int32, (lanes, 128), 1)
    row = jnp.bitwise_and(jnp.right_shift(lane, 1), 31) - step * rows
    col = jnp.bitwise_and(lane, 1) + jnp.where(lane >= 64, 126, 0)
    hit = jnp.where(row * 128 + col == at, 1.0, 0.0).astype(jnp.bfloat16)
    edge_ref[...] += f32dot(feed_ref[...], hit).astype(jnp.bfloat16)


def make_feed(place, arrived, interp, given, blocks=4):
    count, cells, n = interp.shape
    ch = arrived.shape[1]
    lanes = n // blocks
    return pl.pallas_call(
        feed_kernel,
        grid=(blocks,),
        out_shape=(
            jax.ShapeDtypeStruct((FEED, n), jnp.bfloat16),
            jax.ShapeDtypeStruct((FEED, 128), jnp.bfloat16),
        ),
        in_specs=[
            scalars(),
            whole(),
            pl.BlockSpec((count, cells, lanes), lambda i: (0, 0, i)),
            pl.BlockSpec((FEED - NOISY_AT, lanes), lambda i: (0, i)),
        ],
        out_specs=(
            pl.BlockSpec((FEED, lanes), lambda i: (0, i)),
            pl.BlockSpec((FEED, 128), lambda i: (0, 0)),
        ),
        scratch_shapes=[pltpu.VMEM((ch, count * cells), jnp.bfloat16)],
        compiler_params=vmem(),
    )(place, arrived, interp, given)


def strip_kernel(top_ref, bot_ref, edge_ref, left_ref, right_ref):
    wide = jnp.concatenate([top_ref[...], bot_ref[...]], axis=1)
    at = lax.broadcasted_iota(jnp.int32, (512, 128), 0)
    lane = lax.broadcasted_iota(jnp.int32, (512, 128), 1)
    spot = jnp.bitwise_and(lane, 63)
    source = jnp.right_shift(spot, 1) * 128 + jnp.bitwise_and(spot, 1)
    source = source + jnp.where(lane >= 64, 126, 0)
    hit = jnp.where(jnp.logical_and(source == at, spot < 8), 1.0, 0.0).astype(jnp.bfloat16)
    corner = f32dot(wide, hit).astype(jnp.bfloat16)
    edge = edge_ref[...]
    left_ref[...] = jnp.concatenate([edge[:, 0:64], corner[:, 0:64]], axis=1)
    right_ref[...] = jnp.concatenate([edge[:, 64:128], corner[:, 64:128]], axis=1)


def strips(top, bot, edge):
    shape = jax.ShapeDtypeStruct((FEED, 128), jnp.bfloat16)
    return pl.pallas_call(
        strip_kernel,
        out_shape=(shape, shape),
        in_specs=[whole()] * 3,
        out_specs=(whole(), whole()),
        compiler_params=vmem(),
    )(top, bot, edge)


def tap_offset(tap):
    return (tap // 3 - 1) * PITCH + tap % 3 - 1


def net_kernel(
    feed_ref,
    top_ref,
    bot_ref,
    left_ref,
    right_ref,
    mask_ref,
    w_first_ref,
    w_one_ref,
    w_one_back_ref,
    w_two_ref,
    w_two_back_ref,
    w_out_ref,
    w_cond_ref,
    pred_ref,
    dcond_ref,
    grads_ref,
    x_ref,
    a_zero_ref,
    d_two_ref,
    a_one_ref,
    d_one_ref,
    slope_zero_ref,
    sum_one_ref,
    sum_two_ref,
    sum_in_ref,
    sum_out_ref,
    pred_wide_ref,
    dcond_wide_ref,
):
    rows = pred_ref.shape[1]
    ch = 128
    x_ref[:, HIGH * PITCH :] = jnp.zeros((FEED, SPAN - HIGH * PITCH), jnp.bfloat16)
    left = left_ref[...]
    right = right_ref[...]
    for r in range(HIGH):
        if r < 2:
            body = top_ref[:, r * 128 : (r + 1) * 128]
            spot = 64 + 2 * r
        elif r < rows + 2:
            body = feed_ref[:, (r - 2) * 128 : (r - 1) * 128]
            spot = 2 * (r - 2)
        else:
            body = bot_ref[:, (r - rows - 2) * 128 : (r - rows - 1) * 128]
            spot = 68 + 2 * (r - rows - 2)
        line = jnp.concatenate([left[:, spot : spot + 2], body, right[:, spot : spot + 2]], axis=1)
        x_ref[:, r * PITCH : (r + 1) * PITCH] = line
    for ref in (a_zero_ref, d_two_ref, a_one_ref, d_one_ref):
        ref[:, 0:GUARD] = jnp.zeros((ch, GUARD), jnp.bfloat16)
        ref[:, GUARD + SPAN :] = jnp.zeros((ch, GUARD), jnp.bfloat16)
    for ref in (sum_one_ref, sum_two_ref, sum_in_ref, sum_out_ref):
        ref[...] = jnp.zeros_like(ref)

    def at(i, shift=0, extra=0):
        return pl.ds(pl.multiple_of(i * STEP + shift, 128), STEP + extra)

    def taps(ref, i, sign):
        window = ref[:, at(i, 0, 2 * GUARD)]
        pieces = []
        for tap in range(9):
            start = GUARD + sign * tap_offset(tap)
            pieces.append(window[:, start : start + STEP])
        return jnp.concatenate(pieces, axis=0)

    def first(i, carry):
        both = f32dot(w_first_ref[...], x_ref[:, at(i)])
        h_zero = both[0:ch]
        sig = jax.nn.sigmoid(h_zero)
        a_zero_ref[:, at(i, GUARD)] = (h_zero * sig).astype(jnp.bfloat16)
        slope_zero_ref[:, at(i)] = sig * (1.0 + h_zero * (1.0 - sig))
        d_two_ref[:, at(i, GUARD)] = both[ch:].astype(jnp.bfloat16)
        return carry

    lax.fori_loop(0, STEPS, first, 0)

    def second(i, carry):
        inside = mask_ref[0:1, at(i)]
        z_one = f32dot(w_one_ref[...], taps(a_zero_ref, i, 1))
        sig = jax.nn.sigmoid(z_one)
        a_one_ref[:, at(i, GUARD)] = (z_one * sig * inside).astype(jnp.bfloat16)
        slope = sig * (1.0 + z_one * (1.0 - sig))
        back = f32dot(w_two_back_ref[...], taps(d_two_ref, i, -1))
        d_one_ref[:, at(i, GUARD)] = (back * slope * inside).astype(jnp.bfloat16)
        return carry

    lax.fori_loop(0, STEPS, second, 0)

    def third(i, carry):
        own = mask_ref[1:2, at(i)]
        x = x_ref[:, at(i)]
        d_two = d_two_ref[:, at(i, GUARD)].astype(jnp.float32)
        cols_one = taps(a_one_ref, i, 1)
        z_two = f32dot(w_two_ref[...], cols_one)
        a_two = (a_zero_ref[:, at(i, GUARD)].astype(jnp.float32) + z_two).astype(jnp.bfloat16)
        pred_wide_ref[:, at(i)] = f32dot(w_out_ref[...], a_two)
        a_two_own = (a_two.astype(jnp.float32) * own).astype(jnp.bfloat16)
        sum_out_ref[...] += lax.dot_general(a_two_own, x, NT, preferred_element_type=jnp.float32)
        d_two_own = (d_two * own).astype(jnp.bfloat16)
        sum_two_ref[...] += lax.dot_general(
            d_two_own, cols_one, NT, preferred_element_type=jnp.float32
        )
        back = f32dot(w_one_back_ref[...], taps(d_one_ref, i, -1))
        d_zero = ((back + d_two) * slope_zero_ref[:, at(i)] * own).astype(jnp.bfloat16)
        sum_in_ref[...] += lax.dot_general(d_zero, x, NT, preferred_element_type=jnp.float32)
        dcond_wide_ref[:, at(i)] = f32dot(w_cond_ref[...], d_zero)
        d_one_own = (d_one_ref[:, at(i, GUARD)].astype(jnp.float32) * own).astype(jnp.bfloat16)
        sum_one_ref[...] += lax.dot_general(
            d_one_own, taps(a_zero_ref, i, 1), NT, preferred_element_type=jnp.float32
        )
        return carry

    lax.fori_loop(0, STEPS, third, 0)

    for r in range(rows):
        start = (r + 2) * PITCH + 2
        pred_ref[:, r, :] = pred_wide_ref[0 : pred_ref.shape[0], start : start + 128]
        dcond_ref[:, r * 128 : (r + 1) * 128] = dcond_wide_ref[
            :, start : start + 128
        ].astype(jnp.bfloat16)
    for tap in range(9):
        lanes = slice(tap * 128, (tap + 1) * 128)
        grads_ref[tap * 128 : (tap + 1) * 128, :] = sum_two_ref[:, lanes].astype(jnp.bfloat16)
        grads_ref[(9 + tap) * 128 : (10 + tap) * 128, :] = sum_one_ref[:, lanes].astype(
            jnp.bfloat16
        )
    grads_ref[2304:2560, :] = jnp.zeros((256, 128), jnp.bfloat16)
    grads_ref[2304:2432, 0:FEED] = sum_in_ref[...].astype(jnp.bfloat16)
    grads_ref[2432:2560, 0:FEED] = sum_out_ref[...].astype(jnp.bfloat16)
    grads_ref[2560:, :] = jnp.zeros((128 * CHUNK - 2560, 128), jnp.bfloat16)


def net(chans, rows, cols, args):
    ch = 128
    wide = SPAN + 2 * GUARD
    bf, f32 = jnp.bfloat16, jnp.float32
    return pl.pallas_call(
        net_kernel,
        out_shape=(
            jax.ShapeDtypeStruct((chans, rows, cols), f32),
            jax.ShapeDtypeStruct((48, rows * cols), bf),
            jax.ShapeDtypeStruct((128 * CHUNK, 128), bf),
        ),
        in_specs=[whole()] * len(args),
        out_specs=(whole(),) * 3,
        scratch_shapes=[
            pltpu.VMEM((FEED, SPAN), bf),
            pltpu.VMEM((ch, wide), bf),
            pltpu.VMEM((ch, wide), bf),
            pltpu.VMEM((ch, wide), bf),
            pltpu.VMEM((ch, wide), bf),
            pltpu.VMEM((ch, SPAN), f32),
            pltpu.VMEM((ch, 9 * ch), f32),
            pltpu.VMEM((ch, 9 * ch), f32),
            pltpu.VMEM((ch, FEED), f32),
            pltpu.VMEM((ch, FEED), f32),
            pltpu.VMEM((16, SPAN), f32),
            pltpu.VMEM((48, SPAN), f32),
        ],
        compiler_params=vmem(),
    )(*args)


def block_kernel(place_ref, dcond_ref, interp_ref, out_ref, total):
    step = pl.program_id(0)
    count, cells, lanes = interp_ref.shape
    ch = out_ref.shape[1]
    matrix = interp_ref[...].reshape(count * cells, lanes)
    part = lax.dot_general(dcond_ref[...], matrix, NT, preferred_element_type=jnp.float32)

    @pl.when(step == 0)
    def _():
        total[...] = part

    @pl.when(step > 0)
    def _():
        total[...] += part

    @pl.when(step == pl.num_programs(0) - 1)
    def _():
        out_ref[...] = jnp.zeros_like(out_ref)
        for j in range(count):
            out_ref[place_ref[j]] = total[0:ch, j * cells : (j + 1) * cells].astype(jnp.bfloat16)


def blocks_back(place, dcond, interp, slots, ch, blocks=4):
    count, cells, n = interp.shape
    lanes = n // blocks
    return pl.pallas_call(
        block_kernel,
        grid=(blocks,),
        out_shape=jax.ShapeDtypeStruct((slots, ch, cells), jnp.bfloat16),
        in_specs=[
            scalars(),
            pl.BlockSpec((dcond.shape[0], lanes), lambda i: (0, i)),
            pl.BlockSpec((count, cells, lanes), lambda i: (0, 0, i)),
        ],
        out_specs=pl.BlockSpec((slots, ch, cells), lambda i: (0, 0, 0)),
        scratch_shapes=[pltpu.VMEM((dcond.shape[0], count * cells), jnp.float32)],
        compiler_params=vmem(),
    )(place, dcond, interp)


def gather_kernel(asked_ref, returned_ref, out_ref, total):
    total[...] = jnp.zeros_like(total)
    for i in range(returned_ref.shape[0]):
        slot = asked_ref[i]

        @pl.when(slot >= 0)
        def _(slot=slot, i=i):
            total[slot] += returned_ref[i].astype(jnp.float32)

    out_ref[...] = total[...].astype(jnp.bfloat16)


def band_blocks(asked, returned, per_band):
    shape = (per_band,) + returned.shape[1:]
    return pl.pallas_call(
        gather_kernel,
        out_shape=jax.ShapeDtypeStruct(shape, jnp.bfloat16),
        in_specs=[scalars(), whole()],
        out_specs=whole(),
        scratch_shapes=[pltpu.VMEM(shape, jnp.float32)],
        compiler_params=vmem(),
    )(asked, returned)


def block_sum_kernel(parts_ref, out_ref):
    total = parts_ref[0].astype(jnp.float32)
    for i in range(1, parts_ref.shape[0]):
        total = total + parts_ref[i].astype(jnp.float32)
    out_ref[...] = total


def block_sum(parts):
    return pl.pallas_call(
        block_sum_kernel,
        out_shape=jax.ShapeDtypeStruct(parts.shape[1:], jnp.float32),
        in_specs=[whole()],
        out_specs=whole(),
        compiler_params=vmem(),
    )(parts)


def share_kernel(parts_ref, out_ref):
    total = parts_ref[0].astype(jnp.float32)
    for i in range(1, parts_ref.shape[0]):
        total = total + parts_ref[i].astype(jnp.float32)
    out_ref[...] = jnp.broadcast_to(total.astype(jnp.bfloat16)[None], out_ref.shape)


def share(parts):
    return pl.pallas_call(
        share_kernel,
        out_shape=jax.ShapeDtypeStruct(parts.shape, jnp.bfloat16),
        in_specs=[whole()],
        out_specs=whole(),
        compiler_params=vmem(),
    )(parts)


def final_kernel(factor, parts_ref, in_ref, one_ref, two_ref, out_ref):
    ch = in_ref.shape[0]
    side = two_ref.shape[0]
    for tap in range(9):
        two_ref[tap // side, tap % side] = (
            parts_ref[tap * ch : (tap + 1) * ch, :].astype(jnp.float32) * factor
        )
        one_ref[tap // side, tap % side] = (
            parts_ref[(9 + tap) * ch : (10 + tap) * ch, :].astype(jnp.float32) * factor
        )
    first = parts_ref[18 * ch : 19 * ch, :].astype(jnp.float32) * factor
    chans = out_ref.shape[0]
    coarse_ch = in_ref.shape[1] - chans
    in_ref[:, 0:coarse_ch] = first[:, 0:coarse_ch]
    in_ref[:, coarse_ch:] = first[:, NOISY_AT : NOISY_AT + chans]
    last = parts_ref[19 * ch : 20 * ch, :].astype(jnp.float32) * factor
    out_ref[...] = last.T[GRAD_AT : GRAD_AT + chans, :]


def final(parts, width, taps, inner, chans, factor):
    f32 = jnp.float32
    return pl.pallas_call(
        functools.partial(final_kernel, factor),
        out_shape=(
            jax.ShapeDtypeStruct((width, inner), f32),
            jax.ShapeDtypeStruct(taps, f32),
            jax.ShapeDtypeStruct(taps, f32),
            jax.ShapeDtypeStruct((chans, width), f32),
        ),
        in_specs=[whole()],
        out_specs=(whole(),) * 4,
        compiler_params=vmem(),
    )(parts)


def halo(first, last, axis):
    count = lax.axis_size(axis)
    up = [(i, i + 1) for i in range(count - 1)]
    down = [(i + 1, i) for i in range(count - 1)]
    return lax.ppermute(last, axis, up), lax.ppermute(first, axis, down)


def cell_masks(rows, cols, n_tile, n_band):
    flat = np.arange(SPAN)
    row = flat // PITCH
    col = flat % PITCH
    own = (row >= 2) & (row < rows + 2) & (col >= 2) & (col < cols + 2)
    grid_row = lax.axis_index("tile") * rows + (row - 2)
    grid_col = lax.axis_index("band") * cols + (col - 2)
    inside = (
        (grid_row >= 0)
        & (grid_row < rows * n_tile)
        & (grid_col >= 0)
        & (grid_col < cols * n_band)
    )
    masks = jnp.stack([inside.astype(jnp.float32), jnp.asarray(own, jnp.float32)])
    return jnp.pad(masks, ((0, 6), (0, 0)))


def per_device(
    noisy, grad_pred, coarse, margin_band, margin_slot, interp, w_in, w_conv1, w_conv2, w_out
):
    width = w_in.shape[0]
    chans, rows, cols = noisy.shape
    cells = rows * cols
    coarse_ch = coarse.shape[2]
    per_band = coarse.shape[1]
    n_band = lax.axis_size("band")
    n_tile = lax.axis_size("tile")
    slots = n_band * MOST
    local_interp = interp[0, 0]

    place, wanted = plan(margin_band.reshape(-1), margin_slot, slots)
    asked = lax.all_to_all(
        wanted.reshape(n_band, MOST), "band", split_axis=0, concat_axis=0, tiled=True
    ).reshape(slots)
    served = serve(asked, coarse[0])
    arrived = lax.all_to_all(served, "band", split_axis=0, concat_axis=0, tiled=True)

    given = jnp.concatenate(
        [
            noisy.reshape(chans, cells),
            grad_pred.reshape(chans, cells),
            jnp.zeros((FEED - NOISY_AT - 2 * chans, cells), jnp.bfloat16),
        ],
        0,
    )
    w_pad = lambda w, before: jnp.pad(w, ((0, 0), (before, FEED - before - w.shape[1])))
    w_first = jnp.concatenate(
        [
            w_pad(w_in[:, :coarse_ch], 0) + w_pad(w_in[:, coarse_ch:], NOISY_AT),
            w_pad(w_out.T, GRAD_AT),
        ],
        0,
    )
    forward = lambda w: w.transpose(2, 0, 1, 3).reshape(width, 9 * width)
    backward = lambda w: w.transpose(3, 0, 1, 2).reshape(width, 9 * width)
    masks = cell_masks(rows, cols, n_tile, n_band)

    feed, edge = make_feed(place, arrived, local_interp, given)
    top, bot = halo(feed[:, : 2 * cols], feed[:, cells - 2 * cols :], "tile")
    left_out, right_out = strips(top, bot, edge)
    left, right = halo(left_out, right_out, "band")
    pred, dcond, grads = net(
        chans,
        rows,
        cols,
        (
            feed,
            top,
            bot,
            left,
            right,
            masks,
            w_first,
            forward(w_conv1),
            backward(w_conv1),
            forward(w_conv2),
            backward(w_conv2),
            jnp.pad(w_out, ((0, 16 - chans), (0, 0))),
            jnp.pad(w_in[:, :coarse_ch].T, ((0, 48 - coarse_ch), (0, 0))),
        ),
    )
    grads = lax.all_to_all(
        grads.reshape(n_tile * n_band, CHUNK, 128), ALL, split_axis=0, concat_axis=0, tiled=True
    )
    outgoing = blocks_back(place, dcond, local_interp, slots, coarse_ch)
    returned = lax.all_to_all(outgoing, "band", split_axis=0, concat_axis=0, tiled=True)
    summed = lax.all_to_all(share(grads), ALL, split_axis=0, concat_axis=0, tiled=True)
    owned = band_blocks(asked, returned, per_band)
    mine = lax.all_to_all(owned, "tile", split_axis=0, concat_axis=0, tiled=True)
    coarse_grad = block_sum(
        mine.reshape((n_tile, 1, per_band // n_tile) + coarse.shape[2:])
    )
    factor = 1.0 / math.sqrt(cells * n_tile * n_band)
    grad_in, grad_one, grad_two, grad_out = final(
        summed.reshape(-1, 128), width, w_conv1.shape, w_in.shape[1], chans, factor
    )
    return (pred, coarse_grad, grad_in, grad_one, grad_two, grad_out)


def solution(mesh):
    placed = (
        P(None, "tile", "band"),
        P(None, "tile", "band"),
        P("band", None, None, None),
        P(("tile", "band"), None),
        P(("tile", "band")),
        P("tile", "band", None, None, None),
        P(),
        P(),
        P(),
        P(),
    )
    return jax.shard_map(
        per_device,
        mesh=mesh,
        in_specs=placed,
        out_specs=(P(None, "tile", "band"), P("band", "tile", None, None), P(), P(), P(), P()),
        check_vma=False,
    )
```

```python
import functools
import math

import jax
import jax.numpy as jnp
from jax import lax
from jax.experimental import pallas as pl
from jax.experimental.pallas import tpu as pltpu
from jax.sharding import PartitionSpec as P

MOST = 4
ALL = ("tile", "band")

FEED = 80
NOISY_AT = 48
GRAD_AT = 60
WIDE = 48
SUMS = 2560
OUT_AT = 80
LOW, HIGH = 40, 112
CHUNK = 24
NT = (((1,), (1,)), ((), ()))


def f32dot(left, right):
    return jnp.dot(left, right, preferred_element_type=jnp.float32)


def vmem(limit=56 * 1024 * 1024):
    return pltpu.CompilerParams(vmem_limit_bytes=limit)


def whole():
    return pl.BlockSpec(memory_space=pltpu.VMEM)


def scalars():
    return pl.BlockSpec(memory_space=pltpu.SMEM)


def plan_kernel(band_ref, slot_ref, place_ref, wanted_ref):
    count = slot_ref.shape[0]
    for i in range(wanted_ref.shape[0]):
        wanted_ref[i] = jnp.int32(-1)
    for j in range(count):
        band = band_ref[j]
        rank = jnp.int32(0)
        for i in range(j):
            rank = rank + jnp.where(band_ref[i] == band, 1, 0)
        place = band * MOST + rank
        place_ref[j] = place
        wanted_ref[place] = slot_ref[j]


def plan(bands, slots, total):
    return pl.pallas_call(
        plan_kernel,
        out_shape=(
            jax.ShapeDtypeStruct(slots.shape, jnp.int32),
            jax.ShapeDtypeStruct((total,), jnp.int32),
        ),
        in_specs=[scalars(), scalars()],
        out_specs=(scalars(), scalars()),
    )(bands, slots)


def serve_kernel(asked_ref, coarse_ref, out_ref):
    for i in range(out_ref.shape[0]):
        out_ref[i] = coarse_ref[jnp.maximum(asked_ref[i], 0)]


def serve(asked, coarse):
    return pl.pallas_call(
        serve_kernel,
        out_shape=jax.ShapeDtypeStruct((asked.shape[0],) + coarse.shape[1:], coarse.dtype),
        in_specs=[scalars(), whole()],
        out_specs=whole(),
        compiler_params=vmem(),
    )(asked, coarse)


def feed_kernel(place_ref, arrived_ref, interp_ref, given_ref, feed_ref, edge_ref, picked):
    step = pl.program_id(0)
    ch = arrived_ref.shape[1]
    count = interp_ref.shape[0]
    cells = interp_ref.shape[1]
    lanes = interp_ref.shape[2]

    @pl.when(step == 0)
    def _():
        edge_ref[...] = jnp.zeros_like(edge_ref)
        for j in range(count):
            picked[:, j * cells : (j + 1) * cells] = arrived_ref[place_ref[j]]

    matrix = interp_ref[...].reshape(count * cells, lanes)
    cond = f32dot(picked[...], matrix).astype(jnp.bfloat16)
    feed_ref[...] = jnp.zeros_like(feed_ref)
    feed_ref[0:ch, :] = cond
    feed_ref[NOISY_AT:, :] = given_ref[...]
    rows = lanes // 128
    at = lax.broadcasted_iota(jnp.int32, (lanes, 256), 0)
    lane = lax.broadcasted_iota(jnp.int32, (lanes, 256), 1)
    row = jnp.bitwise_and(lane, 63) - 2 - step * rows
    kind = jnp.right_shift(lane, 6)
    col = kind + jnp.where(kind >= 2, 124, 0)
    hit = jnp.where(row * 128 + col == at, 1.0, 0.0).astype(jnp.bfloat16)
    edge_ref[...] += f32dot(feed_ref[...], hit).astype(jnp.bfloat16)


def make_feed(place, arrived, interp, given, blocks=4):
    count, cells, n = interp.shape
    ch = arrived.shape[1]
    lanes = n // blocks
    return pl.pallas_call(
        feed_kernel,
        grid=(blocks,),
        out_shape=(
            jax.ShapeDtypeStruct((FEED, n), jnp.bfloat16),
            jax.ShapeDtypeStruct((FEED, 256), jnp.bfloat16),
        ),
        in_specs=[
            scalars(),
            whole(),
            pl.BlockSpec((count, cells, lanes), lambda i: (0, 0, i)),
            pl.BlockSpec((FEED - NOISY_AT, lanes), lambda i: (0, i)),
        ],
        out_specs=(
            pl.BlockSpec((FEED, lanes), lambda i: (0, i)),
            pl.BlockSpec((FEED, 256), lambda i: (0, 0)),
        ),
        scratch_shapes=[pltpu.VMEM((ch, count * cells), jnp.bfloat16)],
        compiler_params=vmem(),
    )(place, arrived, interp, given)


def strip_kernel(top_ref, bot_ref, edge_ref, left_ref, right_ref, own_ref):
    wide = jnp.concatenate([top_ref[...], bot_ref[...]], axis=1)
    at = lax.broadcasted_iota(jnp.int32, (512, 256), 0)
    lane = lax.broadcasted_iota(jnp.int32, (512, 256), 1)
    spot = jnp.bitwise_and(lane, 63)
    row = jnp.where(spot < 2, spot, jnp.where(jnp.logical_or(spot == 34, spot == 35), spot - 32, 8))
    kind = jnp.right_shift(lane, 6)
    col = kind + jnp.where(kind >= 2, 124, 0)
    hit = jnp.where(row * 128 + col == at, 1.0, 0.0).astype(jnp.bfloat16)
    edge = (edge_ref[...].astype(jnp.float32) + f32dot(wide, hit)).astype(jnp.bfloat16)
    left_ref[...] = edge[:, 0:128]
    right_ref[...] = edge[:, 128:256]
    own_ref[...] = jnp.concatenate([edge[:, 0:64], edge[:, 192:256]], axis=1)


def strips(top, bot, edge):
    shape = jax.ShapeDtypeStruct((FEED, 128), jnp.bfloat16)
    return pl.pallas_call(
        strip_kernel,
        out_shape=(shape,) * 3,
        in_specs=[whole()] * 3,
        out_specs=(whole(),) * 3,
        compiler_params=vmem(),
    )(top, bot, edge)


def silu_parts(value):
    sig = jax.nn.sigmoid(value)
    return value * sig, sig * (1.0 + value * (1.0 - sig))


def net_kernel(
    place_ref,
    flag_ref,
    feed_ref,
    top_ref,
    bot_ref,
    left_ref,
    right_ref,
    own_ref,
    w_first_ref,
    w_one_ref,
    w_one_back_ref,
    w_two_ref,
    w_two_back_ref,
    w_out_ref,
    w_cond_ref,
    interp_ref,
    pred_ref,
    pack_ref,
    x_ref,
    a_zero_ref,
    d_two_ref,
    a_one_ref,
    d_one_ref,
    slope_ref,
    sum_one_ref,
    sum_two_ref,
    dcond_ref,
    matrix_ref,
    sem,
):
    rows = pred_ref.shape[1]
    tall = rows + 4
    ch = 128
    bf, f32 = jnp.bfloat16, jnp.float32
    fetch = pltpu.make_async_copy(interp_ref, matrix_ref, sem)
    fetch.start()
    lane = lax.broadcasted_iota(jnp.int32, (ch, 128), 1)
    at_left = lane == 0
    at_right = lane == 127

    def put(ref, row, value, edge, edge_row):
        lanes = slice(row * 128, (row + 1) * 128)
        value = value.astype(f32)
        left = pltpu.roll(edge, (128 - edge_row) % 128, 1)
        right = pltpu.roll(edge, 63 - edge_row, 1)
        ref[0:ch, lanes] = jnp.where(at_left, left, pltpu.roll(value, 1, 1)).astype(bf)
        ref[ch : 2 * ch, lanes] = value.astype(bf)
        ref[2 * ch :, lanes] = jnp.where(at_right, right, pltpu.roll(value, 127, 1)).astype(bf)

    def around(ref, row, count):
        return jnp.concatenate(
            [ref[:, (row + p) * 128 : (row + p + count) * 128] for p in range(3)], axis=0
        )

    left, right, own = left_ref[...], right_ref[...], own_ref[...]
    groups = (
        jnp.concatenate([left[:, 0:64], own[:, 64:128]], axis=1),
        jnp.concatenate([left[:, 64:128], right[:, 0:64]], axis=1),
        jnp.concatenate([own[:, 0:64], right[:, 64:128]], axis=1),
    )
    edge_x = jnp.concatenate(groups, axis=1)
    both = f32dot(w_first_ref[...], edge_x)
    edge_a = silu_parts(both[0:ch])[0].astype(bf).astype(f32)
    edge_d = both[ch:].astype(bf).astype(f32)

    def edge_taps(field):
        pieces = []
        for p in range(3):
            for q in range(3):
                part = field[:, q * 128 : (q + 1) * 128]
                pieces.append(part if p == 1 else pltpu.roll(part, (1 - p) % 128, 1))
        return jnp.concatenate(pieces, axis=0).astype(bf)

    spot = jnp.bitwise_and(lane, 63)
    edge_in = jnp.where(lane >= 64, flag_ref[3], flag_ref[2])
    edge_in = edge_in * jnp.where(spot == 1, flag_ref[0], 1.0)
    edge_in = edge_in * jnp.where(spot == rows + 2, flag_ref[1], 1.0)
    edge_act, edge_slope = silu_parts(f32dot(w_one_ref[...], edge_taps(edge_a)))
    edge_a_one = (edge_act * edge_in).astype(bf).astype(f32)
    edge_back = f32dot(w_two_back_ref[...], edge_taps(edge_d))
    edge_d_one = (edge_back * edge_slope * edge_in).astype(bf).astype(f32)
    edge_a = edge_a[:, 128:256]
    edge_d = edge_d[:, 128:256]

    x_ref[:, 0:256] = top_ref[...]
    x_ref[:, 256 : (rows + 2) * 128] = feed_ref[...]
    x_ref[:, (rows + 2) * 128 :] = bot_ref[...]
    for row in range(0, tall, 4):
        both = f32dot(w_first_ref[...], x_ref[:, row * 128 : (row + 4) * 128])
        act, slope = silu_parts(both[0:ch])
        slope_ref[:, row * 128 : (row + 4) * 128] = slope
        for k in range(4):
            lanes = slice(k * 128, (k + 1) * 128)
            put(a_zero_ref, row + k, act[:, lanes], edge_a, row + k)
            put(d_two_ref, row + k, both[ch:, lanes], edge_d, row + k)

    half = (rows + 2) // 2
    for row in (0, half):
        act, slope = silu_parts(f32dot(w_one_ref[...], around(a_zero_ref, row, half)))
        back = f32dot(w_two_back_ref[...], around(d_two_ref, row, half)) * slope
        for k in range(half):
            lanes = slice(k * 128, (k + 1) * 128)
            act_row, back_row = act[:, lanes], back[:, lanes]
            if row + k == 0:
                act_row, back_row = act_row * flag_ref[0], back_row * flag_ref[0]
            if row + k == rows + 1:
                act_row, back_row = act_row * flag_ref[1], back_row * flag_ref[1]
            put(a_one_ref, row + k, act_row, edge_a_one, row + k + 1)
            put(d_one_ref, row + k, back_row, edge_d_one, row + k + 1)

    half = rows // 2
    sum_in = jnp.zeros((ch, FEED), f32)
    sum_out = jnp.zeros((ch, FEED - NOISY_AT), f32)
    for row in (0, half):
        mine = slice((row + 2) * 128, (row + 2 + half) * 128)
        inner = slice((row + 1) * 128, (row + 1 + half) * 128)
        x = x_ref[:, mine]
        d_two = d_two_ref[ch : 2 * ch, mine]
        cols_one = around(a_one_ref, row, half)
        z_two = f32dot(w_two_ref[...], cols_one)
        a_two = (a_zero_ref[ch : 2 * ch, mine].astype(f32) + z_two).astype(bf)
        pred = f32dot(w_out_ref[...], a_two)
        for k in range(half):
            pred_ref[:, row + k, :] = pred[0 : pred_ref.shape[0], k * 128 : (k + 1) * 128]
        sum_out = sum_out + nt_dot(a_two, x[NOISY_AT:, :])
        part_two = nt_dot(d_two, cols_one)
        back = f32dot(w_one_back_ref[...], around(d_one_ref, row, half))
        d_zero = ((back + d_two.astype(f32)) * slope_ref[:, mine]).astype(bf)
        sum_in = sum_in + nt_dot(d_zero, x)
        dcond_ref[:, row * 128 : (row + half) * 128] = f32dot(w_cond_ref[...], d_zero).astype(bf)
        part_one = nt_dot(d_one_ref[ch : 2 * ch, inner], around(a_zero_ref, row + 1, half))
        if row == 0:
            sum_two_ref[...] = part_two
            sum_one_ref[...] = part_one
        else:
            sum_two_ref[...] += part_two
            sum_one_ref[...] += part_one

    bands = pack_ref.shape[0]
    share_rows = SUMS // bands

    def store(first, value):
        done = 0
        while done < value.shape[0]:
            band, spot = divmod(first + done, share_rows)
            count = min(value.shape[0] - done, share_rows - spot)
            pack_ref[band, spot : spot + count, :] = value[done : done + count, :]
            done += count

    for tap in range(9):
        lanes = slice(tap * 128, (tap + 1) * 128)
        store(tap * ch, sum_two_ref[:, lanes].astype(bf))
        store((9 + tap) * ch, sum_one_ref[:, lanes].astype(bf))
    pad = jnp.zeros((ch, 128 - OUT_AT - (FEED - NOISY_AT)), f32)
    store(18 * ch, jnp.concatenate([sum_in, sum_out, pad], axis=1).astype(bf))
    store(19 * ch, jnp.zeros((ch, 128), bf))
    for band in range(bands):
        pack_ref[band, share_rows:, :] = jnp.zeros((MOST * WIDE, 128), bf)
    fetch.wait()
    count, cells, n = matrix_ref.shape
    blocks = nt_dot(dcond_ref[...], matrix_ref[...].reshape(count * cells, n)).astype(bf)
    for j in range(count):
        place = place_ref[j]
        spot = share_rows + jnp.bitwise_and(place, MOST - 1) * WIDE
        pack_ref[jnp.right_shift(place, 2), pl.ds(pl.multiple_of(spot, 16), WIDE), :] = blocks[
            :, j * cells : (j + 1) * cells
        ]


def nt_dot(left, right):
    return lax.dot_general(left, right, NT, preferred_element_type=jnp.float32)


def net(chans, rows, cols, n_band, args):
    ch = 128
    bf, f32 = jnp.bfloat16, jnp.float32
    tall = (rows + 4) * cols
    inner = (rows + 2) * cols
    interp = args[-1]
    return pl.pallas_call(
        net_kernel,
        out_shape=(
            jax.ShapeDtypeStruct((chans, rows, cols), f32),
            jax.ShapeDtypeStruct((n_band, SUMS // n_band + MOST * WIDE, 128), bf),
        ),
        in_specs=[scalars(), scalars()]
        + [whole()] * (len(args) - 3)
        + [pl.BlockSpec(memory_space=pl.ANY)],
        out_specs=(whole(),) * 2,
        scratch_shapes=[
            pltpu.VMEM((FEED, tall), bf),
            pltpu.VMEM((3 * ch, tall), bf),
            pltpu.VMEM((3 * ch, tall), bf),
            pltpu.VMEM((3 * ch, inner), bf),
            pltpu.VMEM((3 * ch, inner), bf),
            pltpu.VMEM((ch, tall), f32),
            pltpu.VMEM((ch, 9 * ch), f32),
            pltpu.VMEM((ch, 9 * ch), f32),
            pltpu.VMEM((WIDE, rows * cols), bf),
            pltpu.VMEM(interp.shape, bf),
            pltpu.SemaphoreType.DMA(()),
        ],
        compiler_params=vmem(),
    )(*args)


def merge_kernel(asked_ref, parts_ref, out_ref, total, weights):
    bands = parts_ref.shape[0]
    dests = out_ref.shape[0]
    share_rows = weights.shape[0]
    f32 = jnp.float32
    total[...] = jnp.zeros_like(total)
    whole_sum = parts_ref[0, 0:share_rows, :].astype(f32)
    for band in range(1, bands):
        whole_sum = whole_sum + parts_ref[band, 0:share_rows, :].astype(f32)
    weights[...] = whole_sum
    each = share_rows // dests
    for dest in range(dests):
        total[dest, 2 * LOW : 2 * LOW + each, :] = weights[dest * each : (dest + 1) * each, :]
    for i in range(bands * MOST):
        slot = asked_ref[i]
        start = share_rows + (i % MOST) * WIDE
        block = parts_ref[i // MOST, start : start + WIDE, :].astype(f32)[0:LOW]

        @pl.when(slot >= 0)
        def _(slot=slot, block=block):
            spot = pl.ds(pl.multiple_of(jnp.bitwise_and(slot, 1) * LOW, 8), LOW)
            total[jnp.right_shift(slot, 1), spot, :] += block

    out_ref[...] = total[...].astype(jnp.bfloat16)


def merge(asked, parts, dests):
    return pl.pallas_call(
        merge_kernel,
        out_shape=jax.ShapeDtypeStruct((dests, HIGH, 128), jnp.bfloat16),
        in_specs=[scalars(), whole()],
        out_specs=whole(),
        scratch_shapes=[
            pltpu.VMEM((dests, HIGH, 128), jnp.float32),
            pltpu.VMEM((SUMS // parts.shape[0], 128), jnp.float32),
        ],
        compiler_params=vmem(),
    )(asked, parts)


def share_kernel(parts_ref, block_ref, out_ref, total):
    value = parts_ref[0].astype(jnp.float32)
    for i in range(1, parts_ref.shape[0]):
        value = value + parts_ref[i].astype(jnp.float32)
    total[...] = value
    ch = block_ref.shape[2]
    for k in range(block_ref.shape[1]):
        block_ref[0, k] = total[k * LOW : k * LOW + ch, :]
    chunk = total[2 * LOW : 2 * LOW + CHUNK, :].astype(jnp.bfloat16)
    out_ref[...] = jnp.broadcast_to(chunk[None], out_ref.shape)


def share(parts, block_shape, devices):
    return pl.pallas_call(
        share_kernel,
        out_shape=(
            jax.ShapeDtypeStruct(block_shape, jnp.float32),
            jax.ShapeDtypeStruct((devices, CHUNK, 128), jnp.bfloat16),
        ),
        in_specs=[whole()],
        out_specs=(whole(), whole()),
        scratch_shapes=[pltpu.VMEM((HIGH, 128), jnp.float32)],
        compiler_params=vmem(),
    )(parts)


def final_kernel(factor, n_band, parts_ref, in_ref, one_ref, two_ref, out_ref, total):
    ch = in_ref.shape[0]
    side = two_ref.shape[0]
    devices = parts_ref.shape[0]
    each = SUMS // devices
    for device in range(devices):
        tile, band = divmod(device, n_band)
        first = (band * (devices // n_band) + tile) * each
        total[first : first + each, :] = parts_ref[device].astype(jnp.float32)[0:each] * factor
    for tap in range(9):
        two_ref[tap // side, tap % side] = total[tap * ch : (tap + 1) * ch, :]
        one_ref[tap // side, tap % side] = total[(9 + tap) * ch : (10 + tap) * ch, :]
    last = total[18 * ch : 19 * ch, :]
    chans = out_ref.shape[0]
    coarse_ch = in_ref.shape[1] - chans
    in_ref[:, 0:coarse_ch] = last[:, 0:coarse_ch]
    in_ref[:, coarse_ch:] = last[:, NOISY_AT : NOISY_AT + chans]
    start = OUT_AT + GRAD_AT - NOISY_AT
    out_ref[...] = last.T[start : start + chans, :]


def final(parts, n_band, width, taps, inner, chans, factor):
    f32 = jnp.float32
    return pl.pallas_call(
        functools.partial(final_kernel, factor, n_band),
        out_shape=(
            jax.ShapeDtypeStruct((width, inner), f32),
            jax.ShapeDtypeStruct(taps, f32),
            jax.ShapeDtypeStruct(taps, f32),
            jax.ShapeDtypeStruct((chans, width), f32),
        ),
        in_specs=[whole()],
        out_specs=(whole(),) * 4,
        scratch_shapes=[pltpu.VMEM((SUMS, 128), f32)],
        compiler_params=vmem(),
    )(parts)


def halo(first, last, axis):
    count = lax.axis_size(axis)
    up = [(i, i + 1) for i in range(count - 1)]
    down = [(i + 1, i) for i in range(count - 1)]
    return lax.ppermute(last, axis, up), lax.ppermute(first, axis, down)


def per_device(
    noisy, grad_pred, coarse, margin_band, margin_slot, interp, w_in, w_conv1, w_conv2, w_out
):
    width = w_in.shape[0]
    chans, rows, cols = noisy.shape
    cells = rows * cols
    coarse_ch = coarse.shape[2]
    per_band = coarse.shape[1]
    n_band = lax.axis_size("band")
    n_tile = lax.axis_size("tile")
    slots = n_band * MOST
    local_interp = interp[0, 0]

    place, wanted = plan(margin_band.reshape(-1), margin_slot, slots)
    asked = lax.all_to_all(
        wanted.reshape(n_band, MOST), "band", split_axis=0, concat_axis=0, tiled=True
    ).reshape(slots)
    served = serve(asked, coarse[0])
    arrived = lax.all_to_all(served, "band", split_axis=0, concat_axis=0, tiled=True)

    given = jnp.concatenate(
        [
            noisy.reshape(chans, cells),
            grad_pred.reshape(chans, cells),
            jnp.zeros((FEED - NOISY_AT - 2 * chans, cells), jnp.bfloat16),
        ],
        0,
    )
    w_pad = lambda w, before: jnp.pad(w, ((0, 0), (before, FEED - before - w.shape[1])))
    w_first = jnp.concatenate(
        [
            w_pad(w_in[:, :coarse_ch], 0) + w_pad(w_in[:, coarse_ch:], NOISY_AT),
            w_pad(w_out.T, GRAD_AT),
        ],
        0,
    )
    forward = lambda w: w.transpose(2, 0, 1, 3).reshape(width, 9 * width)
    backward = lambda w: w[::-1, ::-1].transpose(3, 0, 1, 2).reshape(width, 9 * width)
    weights = (
        w_first,
        forward(w_conv1),
        backward(w_conv1),
        forward(w_conv2),
        backward(w_conv2),
        jnp.pad(w_out, ((0, 16 - chans), (0, 0))),
        jnp.pad(w_in[:, :coarse_ch].T, ((0, WIDE - coarse_ch), (0, 0))),
    )
    tile, band = lax.axis_index("tile"), lax.axis_index("band")
    flags = jnp.stack([tile > 0, tile < n_tile - 1, band > 0, band < n_band - 1])
    flags = flags.astype(jnp.float32)
    arrived, weights = lax.optimization_barrier((arrived, weights))

    feed, edge = make_feed(place, arrived, local_interp, given)
    top, bot = halo(feed[:, : 2 * cols], feed[:, cells - 2 * cols :], "tile")
    left_out, right_out, own = strips(top, bot, edge)
    left, right = halo(left_out, right_out, "band")
    pred, pack = net(
        chans,
        rows,
        cols,
        n_band,
        (place, flags, feed, top, bot, left, right, own) + weights + (local_interp,),
    )
    pack = lax.all_to_all(pack, "band", split_axis=0, concat_axis=0, tiled=True)
    parts = lax.all_to_all(
        merge(asked, pack, n_tile), "tile", split_axis=0, concat_axis=0, tiled=True
    )
    coarse_grad, sums = share(
        parts, (1, per_band // n_tile) + coarse.shape[2:], n_tile * n_band
    )
    sums = lax.all_to_all(sums, ALL, split_axis=0, concat_axis=0, tiled=True)
    factor = 1.0 / math.sqrt(cells * n_tile * n_band)
    grad_in, grad_one, grad_two, grad_out = final(
        sums, n_band, width, w_conv1.shape, w_in.shape[1], chans, factor
    )
    return (pred, coarse_grad, grad_in, grad_one, grad_two, grad_out)


def solution(mesh):
    placed = (
        P(None, "tile", "band"),
        P(None, "tile", "band"),
        P("band", None, None, None),
        P(("tile", "band"), None),
        P(("tile", "band")),
        P("tile", "band", None, None, None),
        P(),
        P(),
        P(),
        P(),
    )
    return jax.shard_map(
        per_device,
        mesh=mesh,
        in_specs=placed,
        out_specs=(P(None, "tile", "band"), P("band", "tile", None, None), P(), P(), P(), P()),
        check_vma=False,
    )
```

```python
import functools
import math

import jax
import jax.numpy as jnp
import numpy as np
from jax import lax
from jax.experimental import pallas as pl
from jax.experimental.pallas import tpu as pltpu
from jax.sharding import PartitionSpec as P

MOST = 4
ALL = ("tile", "band")

FEED = 80
NOISY_AT = 48
GRAD_AT = 60
WIDE = 48
SUMS = 2560
OUT_AT = 80
LOW, HIGH = 40, 112
CHUNK = 24
NT = (((1,), (1,)), ((), ()))


def f32dot(left, right):
    return jnp.dot(left, right, preferred_element_type=jnp.float32)


def vmem(mib):
    return pltpu.CompilerParams(vmem_limit_bytes=mib * 1024 * 1024)


def whole():
    return pl.BlockSpec(memory_space=pltpu.VMEM)


def scalars():
    return pl.BlockSpec(memory_space=pltpu.SMEM)


def plan_kernel(band_ref, slot_ref, place_ref, wanted_ref):
    count = slot_ref.shape[0]
    at_band = lax.broadcasted_iota(jnp.int32, wanted_ref.shape, 0)
    at_rank = lax.broadcasted_iota(jnp.int32, wanted_ref.shape, 2)
    wanted = jnp.full(wanted_ref.shape, -1, jnp.int32)
    for j in range(count):
        band = band_ref[j]
        rank = jnp.int32(0)
        for i in range(j):
            rank = rank + jnp.where(band_ref[i] == band, 1, 0)
        place_ref[j] = band * MOST + rank
        hit = jnp.logical_and(at_band == band, at_rank == rank)
        wanted = jnp.where(hit, slot_ref[j], wanted)
    wanted_ref[...] = wanted


def plan(bands, slots, n_band):
    return pl.pallas_call(
        plan_kernel,
        out_shape=(
            jax.ShapeDtypeStruct(slots.shape, jnp.int32),
            jax.ShapeDtypeStruct((n_band, 8, 128), jnp.int32),
        ),
        in_specs=[scalars(), scalars()],
        out_specs=(scalars(), whole()),
    )(bands, slots)


def prep_kernel(
    noisy_ref,
    grad_ref,
    w_in_ref,
    w_out_ref,
    w_one_ref,
    w_two_ref,
    given_ref,
    first_ref,
    one_ref,
    one_back_ref,
    two_ref,
    two_back_ref,
    out_ref,
    cond_ref,
    small,
    noisy_wide,
    grad_wide,
):
    bf, f32 = jnp.bfloat16, jnp.float32
    chans, rows, _ = noisy_ref.shape
    coarse_ch = w_in_ref.shape[0] - chans
    ch = w_in_ref.shape[1]
    small[...] = jnp.zeros_like(small)
    w_in = w_in_ref[...].astype(f32)
    w_out = w_out_ref[...].astype(f32)
    small[0:coarse_ch, 0:ch] = w_in[0:coarse_ch]
    cond_ref[...] = small[0:WIDE, 0:ch].astype(bf)
    small[NOISY_AT : NOISY_AT + chans, 0:ch] = w_in[coarse_ch:]
    small[GRAD_AT : GRAD_AT + chans, ch:] = w_out
    first_ref[...] = small[...].T[:, 0:FEED].astype(bf)
    out_ref[...] = jnp.concatenate([w_out, jnp.zeros((16 - chans, ch), f32)], axis=0).astype(bf)
    for source, straight, back in (
        (w_one_ref, one_ref, one_back_ref),
        (w_two_ref, two_ref, two_back_ref),
    ):
        for tap in range(9):
            lanes = slice(tap * ch, (tap + 1) * ch)
            straight[:, lanes] = source[tap // 3, tap % 3]
            back[:, lanes] = source[2 - tap // 3, 2 - tap % 3].T
    noisy_wide[...] = noisy_ref[...].astype(f32)
    grad_wide[...] = grad_ref[...].astype(f32)
    pad = jnp.zeros((FEED - NOISY_AT - 2 * chans, 128), f32)
    for r in range(rows):
        pieces = [noisy_wide[:, r, :], grad_wide[:, r, :], pad]
        given_ref[:, r * 128 : (r + 1) * 128] = jnp.concatenate(pieces, axis=0).astype(bf)


def prep(noisy, grad_pred, w_in, w_out, w_one, w_two):
    bf = jnp.bfloat16
    chans, rows, cols = noisy.shape
    ch = w_in.shape[0]
    square = jax.ShapeDtypeStruct((ch, 9 * ch), bf)
    return pl.pallas_call(
        prep_kernel,
        out_shape=(
            jax.ShapeDtypeStruct((FEED - NOISY_AT, rows * cols), bf),
            jax.ShapeDtypeStruct((2 * ch, FEED), bf),
            square,
            square,
            square,
            square,
            jax.ShapeDtypeStruct((16, ch), bf),
            jax.ShapeDtypeStruct((WIDE, ch), bf),
        ),
        in_specs=[whole()] * 6,
        out_specs=(whole(),) * 8,
        scratch_shapes=[
            pltpu.VMEM((128, 2 * ch), jnp.float32),
            pltpu.VMEM(noisy.shape, jnp.float32),
            pltpu.VMEM(noisy.shape, jnp.float32),
        ],
        compiler_params=vmem(56),
    )(noisy, grad_pred, w_in.T, w_out, w_one, w_two)


def serve_kernel(asked_ref, coarse_ref, out_ref):
    for i in range(out_ref.shape[0]):
        out_ref[i] = coarse_ref[jnp.maximum(asked_ref[i // MOST, 0, i % MOST], 0)]


def serve(asked, coarse):
    slots = asked.shape[0] * MOST
    return pl.pallas_call(
        serve_kernel,
        out_shape=jax.ShapeDtypeStruct((slots,) + coarse.shape[1:], coarse.dtype),
        in_specs=[scalars(), whole()],
        out_specs=whole(),
        compiler_params=vmem(4),
    )(asked, coarse)


def feed_kernel(
    place_ref, arrived_ref, interp_ref, given_ref, hit_ref, feed_ref, first_ref, last_ref, edge_ref, picked
):
    step = pl.program_id(0)
    ch = arrived_ref.shape[1]
    count = interp_ref.shape[0]
    cells = interp_ref.shape[1]
    lanes = interp_ref.shape[2]

    @pl.when(step == 0)
    def _():
        edge_ref[...] = jnp.zeros_like(edge_ref)
        for j in range(count):
            picked[:, j * cells : (j + 1) * cells] = arrived_ref[place_ref[j]]

    matrix = interp_ref[...].reshape(count * cells, lanes)
    cond = f32dot(picked[...], matrix).astype(jnp.bfloat16)
    feed_ref[...] = jnp.zeros_like(feed_ref)
    feed_ref[0:ch, :] = cond
    feed_ref[NOISY_AT:, :] = given_ref[...]

    @pl.when(step == 0)
    def _():
        first_ref[...] = feed_ref[:, 0:256]

    @pl.when(step == pl.num_programs(0) - 1)
    def _():
        last_ref[...] = feed_ref[:, lanes - 256 :]

    piece = pltpu.roll(f32dot(feed_ref[...], hit_ref[...]), 2 + step * (lanes // 128), 1)
    edge_ref[...] += piece.astype(jnp.bfloat16)


def column_picks(lanes):
    hit = np.zeros((lanes, 256), np.float32)
    for k, col in enumerate((0, 1, 126, 127)):
        for r in range(lanes // 128):
            hit[r * 128 + col, k * 64 + r] = 1.0
    return jnp.asarray(hit, jnp.bfloat16)


def make_feed(place, arrived, interp, given, blocks=4):
    count, cells, n = interp.shape
    ch = arrived.shape[1]
    lanes = n // blocks
    bf = jnp.bfloat16
    return pl.pallas_call(
        feed_kernel,
        grid=(blocks,),
        out_shape=(
            jax.ShapeDtypeStruct((FEED, n), bf),
            jax.ShapeDtypeStruct((FEED, 256), bf),
            jax.ShapeDtypeStruct((FEED, 256), bf),
            jax.ShapeDtypeStruct((FEED, 256), bf),
        ),
        in_specs=[
            scalars(),
            whole(),
            pl.BlockSpec((count, cells, lanes), lambda i: (0, 0, i)),
            pl.BlockSpec((FEED - NOISY_AT, lanes), lambda i: (0, i)),
            whole(),
        ],
        out_specs=(
            pl.BlockSpec((FEED, lanes), lambda i: (0, i)),
            pl.BlockSpec((FEED, 256), lambda i: (0, 0)),
            pl.BlockSpec((FEED, 256), lambda i: (0, 0)),
            pl.BlockSpec((FEED, 256), lambda i: (0, 0)),
        ),
        scratch_shapes=[pltpu.VMEM((ch, count * cells), bf)],
        compiler_params=vmem(56),
    )(place, arrived, interp, given, column_picks(lanes))


def strip_kernel(top_ref, bot_ref, edge_ref, left_ref, right_ref, own_ref):
    wide = jnp.concatenate([top_ref[...], bot_ref[...]], axis=1)
    at = lax.broadcasted_iota(jnp.int32, (512, 256), 0)
    lane = lax.broadcasted_iota(jnp.int32, (512, 256), 1)
    spot = jnp.bitwise_and(lane, 63)
    row = jnp.where(spot < 2, spot, jnp.where(jnp.logical_or(spot == 34, spot == 35), spot - 32, 8))
    kind = jnp.right_shift(lane, 6)
    col = kind + jnp.where(kind >= 2, 124, 0)
    hit = jnp.where(row * 128 + col == at, 1.0, 0.0).astype(jnp.bfloat16)
    edge = (edge_ref[...].astype(jnp.float32) + f32dot(wide, hit)).astype(jnp.bfloat16)
    left_ref[...] = edge[:, 0:128]
    right_ref[...] = edge[:, 128:256]
    own_ref[...] = jnp.concatenate([edge[:, 0:64], edge[:, 192:256]], axis=1)


def strips(top, bot, edge):
    shape = jax.ShapeDtypeStruct((FEED, 128), jnp.bfloat16)
    return pl.pallas_call(
        strip_kernel,
        out_shape=(shape,) * 3,
        in_specs=[whole()] * 3,
        out_specs=(whole(),) * 3,
        compiler_params=vmem(4),
    )(top, bot, edge)


def silu_parts(value):
    sig = jax.nn.sigmoid(value)
    return value * sig, sig * (1.0 + value * (1.0 - sig))


def net_kernel(
    place_ref,
    flag_ref,
    feed_ref,
    top_ref,
    bot_ref,
    left_ref,
    right_ref,
    own_ref,
    w_first_ref,
    w_one_ref,
    w_one_back_ref,
    w_two_ref,
    w_two_back_ref,
    w_out_ref,
    w_cond_ref,
    interp_ref,
    pred_ref,
    pack_ref,
    x_ref,
    a_zero_ref,
    d_two_ref,
    a_one_ref,
    d_one_ref,
    slope_ref,
    sum_one_ref,
    sum_two_ref,
    dcond_ref,
    matrix_ref,
    sem,
):
    rows = pred_ref.shape[1]
    tall = rows + 4
    ch = 128
    bf, f32 = jnp.bfloat16, jnp.float32
    fetch = pltpu.make_async_copy(interp_ref, matrix_ref, sem)
    fetch.start()
    lane = lax.broadcasted_iota(jnp.int32, (ch, 128), 1)
    at_left = lane == 0
    at_right = lane == 127

    def put(ref, row, value, edge, edge_row):
        lanes = slice(row * 128, (row + 1) * 128)
        value = value.astype(f32)
        left = pltpu.roll(edge, (128 - edge_row) % 128, 1)
        right = pltpu.roll(edge, 63 - edge_row, 1)
        ref[0:ch, lanes] = jnp.where(at_left, left, pltpu.roll(value, 1, 1)).astype(bf)
        ref[ch : 2 * ch, lanes] = value.astype(bf)
        ref[2 * ch :, lanes] = jnp.where(at_right, right, pltpu.roll(value, 127, 1)).astype(bf)

    def around(ref, row, count):
        return jnp.concatenate(
            [ref[:, (row + p) * 128 : (row + p + count) * 128] for p in range(3)], axis=0
        )

    left, right, own = left_ref[...], right_ref[...], own_ref[...]
    groups = (
        jnp.concatenate([left[:, 0:64], own[:, 64:128]], axis=1),
        jnp.concatenate([left[:, 64:128], right[:, 0:64]], axis=1),
        jnp.concatenate([own[:, 0:64], right[:, 64:128]], axis=1),
    )
    edge_x = jnp.concatenate(groups, axis=1)
    both = f32dot(w_first_ref[...], edge_x)
    edge_a = silu_parts(both[0:ch])[0].astype(bf).astype(f32)
    edge_d = both[ch:].astype(bf).astype(f32)

    def edge_taps(field):
        pieces = []
        for p in range(3):
            for q in range(3):
                part = field[:, q * 128 : (q + 1) * 128]
                pieces.append(part if p == 1 else pltpu.roll(part, (1 - p) % 128, 1))
        return jnp.concatenate(pieces, axis=0).astype(bf)

    spot = jnp.bitwise_and(lane, 63)
    edge_in = jnp.where(lane >= 64, flag_ref[3], flag_ref[2])
    edge_in = edge_in * jnp.where(spot == 1, flag_ref[0], 1.0)
    edge_in = edge_in * jnp.where(spot == rows + 2, flag_ref[1], 1.0)
    edge_act, edge_slope = silu_parts(f32dot(w_one_ref[...], edge_taps(edge_a)))
    edge_a_one = (edge_act * edge_in).astype(bf).astype(f32)
    edge_back = f32dot(w_two_back_ref[...], edge_taps(edge_d))
    edge_d_one = (edge_back * edge_slope * edge_in).astype(bf).astype(f32)
    edge_a = edge_a[:, 128:256]
    edge_d = edge_d[:, 128:256]

    x_ref[:, 0:256] = top_ref[...]
    x_ref[:, 256 : (rows + 2) * 128] = feed_ref[...]
    x_ref[:, (rows + 2) * 128 :] = bot_ref[...]
    for row in range(0, tall, 4):
        both = f32dot(w_first_ref[...], x_ref[:, row * 128 : (row + 4) * 128])
        act, slope = silu_parts(both[0:ch])
        slope_ref[:, row * 128 : (row + 4) * 128] = slope
        for k in range(4):
            lanes = slice(k * 128, (k + 1) * 128)
            put(a_zero_ref, row + k, act[:, lanes], edge_a, row + k)
            put(d_two_ref, row + k, both[ch:, lanes], edge_d, row + k)

    half = (rows + 2) // 2
    for row in (0, half):
        act, slope = silu_parts(f32dot(w_one_ref[...], around(a_zero_ref, row, half)))
        back = f32dot(w_two_back_ref[...], around(d_two_ref, row, half)) * slope
        for k in range(half):
            lanes = slice(k * 128, (k + 1) * 128)
            act_row, back_row = act[:, lanes], back[:, lanes]
            if row + k == 0:
                act_row, back_row = act_row * flag_ref[0], back_row * flag_ref[0]
            if row + k == rows + 1:
                act_row, back_row = act_row * flag_ref[1], back_row * flag_ref[1]
            put(a_one_ref, row + k, act_row, edge_a_one, row + k + 1)
            put(d_one_ref, row + k, back_row, edge_d_one, row + k + 1)

    half = rows // 2
    sum_in = jnp.zeros((ch, FEED), f32)
    sum_out = jnp.zeros((ch, FEED - NOISY_AT), f32)
    for row in (0, half):
        mine = slice((row + 2) * 128, (row + 2 + half) * 128)
        inner = slice((row + 1) * 128, (row + 1 + half) * 128)
        x = x_ref[:, mine]
        d_two = d_two_ref[ch : 2 * ch, mine]
        cols_one = around(a_one_ref, row, half)
        z_two = f32dot(w_two_ref[...], cols_one)
        a_two = (a_zero_ref[ch : 2 * ch, mine].astype(f32) + z_two).astype(bf)
        pred = f32dot(w_out_ref[...], a_two)
        for k in range(half):
            pred_ref[:, row + k, :] = pred[0 : pred_ref.shape[0], k * 128 : (k + 1) * 128]
        sum_out = sum_out + nt_dot(a_two, x[NOISY_AT:, :])
        part_two = nt_dot(d_two, cols_one)
        back = f32dot(w_one_back_ref[...], around(d_one_ref, row, half))
        d_zero = ((back + d_two.astype(f32)) * slope_ref[:, mine]).astype(bf)
        sum_in = sum_in + nt_dot(d_zero, x)
        dcond_ref[:, row * 128 : (row + half) * 128] = f32dot(w_cond_ref[...], d_zero).astype(bf)
        part_one = nt_dot(d_one_ref[ch : 2 * ch, inner], around(a_zero_ref, row + 1, half))
        if row == 0:
            sum_two_ref[...] = part_two
            sum_one_ref[...] = part_one
        else:
            sum_two_ref[...] += part_two
            sum_one_ref[...] += part_one

    bands = pack_ref.shape[0]
    share_rows = SUMS // bands

    def store(first, value):
        done = 0
        while done < value.shape[0]:
            band, spot = divmod(first + done, share_rows)
            count = min(value.shape[0] - done, share_rows - spot)
            pack_ref[band, spot : spot + count, :] = value[done : done + count, :]
            done += count

    for tap in range(9):
        lanes = slice(tap * 128, (tap + 1) * 128)
        store(tap * ch, sum_two_ref[:, lanes].astype(bf))
        store((9 + tap) * ch, sum_one_ref[:, lanes].astype(bf))
    pad = jnp.zeros((ch, 128 - OUT_AT - (FEED - NOISY_AT)), f32)
    store(18 * ch, jnp.concatenate([sum_in, sum_out, pad], axis=1).astype(bf))
    store(19 * ch, jnp.zeros((ch, 128), bf))
    for band in range(bands):
        pack_ref[band, share_rows:, :] = jnp.zeros((MOST * WIDE, 128), bf)
    fetch.wait()
    count, cells, n = matrix_ref.shape
    blocks = nt_dot(dcond_ref[...], matrix_ref[...].reshape(count * cells, n)).astype(bf)
    for j in range(count):
        place = place_ref[j]
        spot = share_rows + jnp.bitwise_and(place, MOST - 1) * WIDE
        pack_ref[jnp.right_shift(place, 2), pl.ds(pl.multiple_of(spot, 16), WIDE), :] = blocks[
            :, j * cells : (j + 1) * cells
        ]


def nt_dot(left, right):
    return lax.dot_general(left, right, NT, preferred_element_type=jnp.float32)


def net(chans, rows, cols, n_band, args):
    ch = 128
    bf, f32 = jnp.bfloat16, jnp.float32
    tall = (rows + 4) * cols
    inner = (rows + 2) * cols
    interp = args[-1]
    return pl.pallas_call(
        net_kernel,
        out_shape=(
            jax.ShapeDtypeStruct((chans, rows, cols), f32),
            jax.ShapeDtypeStruct((n_band, SUMS // n_band + MOST * WIDE, 128), bf),
        ),
        in_specs=[scalars(), scalars()]
        + [whole()] * (len(args) - 3)
        + [pl.BlockSpec(memory_space=pl.ANY)],
        out_specs=(whole(),) * 2,
        scratch_shapes=[
            pltpu.VMEM((FEED, tall), bf),
            pltpu.VMEM((3 * ch, tall), bf),
            pltpu.VMEM((3 * ch, tall), bf),
            pltpu.VMEM((3 * ch, inner), bf),
            pltpu.VMEM((3 * ch, inner), bf),
            pltpu.VMEM((ch, tall), f32),
            pltpu.VMEM((ch, 9 * ch), f32),
            pltpu.VMEM((ch, 9 * ch), f32),
            pltpu.VMEM((WIDE, rows * cols), bf),
            pltpu.VMEM(interp.shape, bf),
            pltpu.SemaphoreType.DMA(()),
        ],
        compiler_params=vmem(56),
    )(*args)


def merge_kernel(asked_ref, parts_ref, out_ref, total, weights):
    bands = parts_ref.shape[0]
    dests = out_ref.shape[0]
    share_rows = weights.shape[0]
    f32 = jnp.float32
    total[...] = jnp.zeros_like(total)
    whole_sum = parts_ref[0, 0:share_rows, :].astype(f32)
    for band in range(1, bands):
        whole_sum = whole_sum + parts_ref[band, 0:share_rows, :].astype(f32)
    weights[...] = whole_sum
    each = share_rows // dests
    for dest in range(dests):
        total[dest, 2 * LOW : 2 * LOW + each, :] = weights[dest * each : (dest + 1) * each, :]
    for i in range(bands * MOST):
        slot = asked_ref[i // MOST, 0, i % MOST]
        start = share_rows + (i % MOST) * WIDE
        block = parts_ref[i // MOST, start : start + WIDE, :].astype(f32)[0:LOW]

        @pl.when(slot >= 0)
        def _(slot=slot, block=block):
            spot = pl.ds(pl.multiple_of(jnp.bitwise_and(slot, 1) * LOW, 8), LOW)
            total[jnp.right_shift(slot, 1), spot, :] += block

    out_ref[...] = total[...].astype(jnp.bfloat16)


def merge(asked, parts, dests):
    return pl.pallas_call(
        merge_kernel,
        out_shape=jax.ShapeDtypeStruct((dests, HIGH, 128), jnp.bfloat16),
        in_specs=[scalars(), whole()],
        out_specs=whole(),
        scratch_shapes=[
            pltpu.VMEM((dests, HIGH, 128), jnp.float32),
            pltpu.VMEM((SUMS // parts.shape[0], 128), jnp.float32),
        ],
        compiler_params=vmem(12),
    )(asked, parts)


def share_kernel(parts_ref, block_ref, out_ref, total):
    value = parts_ref[0].astype(jnp.float32)
    for i in range(1, parts_ref.shape[0]):
        value = value + parts_ref[i].astype(jnp.float32)
    total[...] = value
    ch = block_ref.shape[2]
    for k in range(block_ref.shape[1]):
        block_ref[0, k] = total[k * LOW : k * LOW + ch, :]
    chunk = total[2 * LOW : 2 * LOW + CHUNK, :].astype(jnp.bfloat16)
    out_ref[...] = jnp.broadcast_to(chunk[None], out_ref.shape)


def share(parts, block_shape, devices):
    return pl.pallas_call(
        share_kernel,
        out_shape=(
            jax.ShapeDtypeStruct(block_shape, jnp.float32),
            jax.ShapeDtypeStruct((devices, CHUNK, 128), jnp.bfloat16),
        ),
        in_specs=[whole()],
        out_specs=(whole(), whole()),
        scratch_shapes=[pltpu.VMEM((HIGH, 128), jnp.float32)],
        compiler_params=vmem(8),
    )(parts)


def final_kernel(factor, n_band, parts_ref, in_ref, one_ref, two_ref, out_ref, total):
    ch = in_ref.shape[1]
    side = two_ref.shape[0]
    devices = parts_ref.shape[0]
    each = SUMS // devices
    for device in range(devices):
        tile, band = divmod(device, n_band)
        first = (band * (devices // n_band) + tile) * each
        total[first : first + each, :] = parts_ref[device].astype(jnp.float32)[0:each] * factor
    for tap in range(9):
        two_ref[tap // side, tap % side] = total[tap * ch : (tap + 1) * ch, :]
        one_ref[tap // side, tap % side] = total[(9 + tap) * ch : (10 + tap) * ch, :]
    last = total[18 * ch : 19 * ch, :]
    chans = out_ref.shape[0]
    coarse_ch = in_ref.shape[0] - chans
    flipped = last.T
    in_ref[0:coarse_ch, :] = flipped[0:coarse_ch, :]
    in_ref[coarse_ch:, :] = flipped[NOISY_AT : NOISY_AT + chans, :]
    start = OUT_AT + GRAD_AT - NOISY_AT
    out_ref[...] = flipped[start : start + chans, :]


def final(parts, n_band, width, taps, inner, chans, factor):
    f32 = jnp.float32
    return pl.pallas_call(
        functools.partial(final_kernel, factor, n_band),
        out_shape=(
            jax.ShapeDtypeStruct((inner, width), f32),
            jax.ShapeDtypeStruct(taps, f32),
            jax.ShapeDtypeStruct(taps, f32),
            jax.ShapeDtypeStruct((chans, width), f32),
        ),
        in_specs=[whole()],
        out_specs=(whole(),) * 4,
        scratch_shapes=[pltpu.VMEM((SUMS, 128), f32)],
        compiler_params=vmem(12),
    )(parts)


def halo(first, last, axis):
    count = lax.axis_size(axis)
    up = [(i, i + 1) for i in range(count - 1)]
    down = [(i + 1, i) for i in range(count - 1)]
    return lax.ppermute(last, axis, up), lax.ppermute(first, axis, down)


def per_device(
    noisy, grad_pred, coarse, margin_band, margin_slot, interp, w_in, w_conv1, w_conv2, w_out
):
    width = w_in.shape[0]
    chans, rows, cols = noisy.shape
    cells = rows * cols
    coarse_ch = coarse.shape[2]
    per_band = coarse.shape[1]
    n_band = lax.axis_size("band")
    n_tile = lax.axis_size("tile")
    local_interp = interp[0, 0]

    place, wanted = plan(margin_band.reshape(-1), margin_slot, n_band)
    asked = lax.all_to_all(wanted, "band", split_axis=0, concat_axis=0, tiled=True)
    prepared = prep(noisy, grad_pred, w_in, w_out, w_conv1, w_conv2)
    asked, prepared = lax.optimization_barrier((asked, prepared))
    given, weights = prepared[0], tuple(prepared[1:])
    served = serve(asked, coarse[0])
    arrived = lax.all_to_all(served, "band", split_axis=0, concat_axis=0, tiled=True)
    tile, band = lax.axis_index("tile"), lax.axis_index("band")
    flags = jnp.stack([tile > 0, tile < n_tile - 1, band > 0, band < n_band - 1])
    flags = flags.astype(jnp.float32)
    arrived, flags = lax.optimization_barrier((arrived, flags))

    feed, first, last, edge = make_feed(place, arrived, local_interp, given)
    top, bot = halo(first, last, "tile")
    left_out, right_out, own = strips(top, bot, edge)
    left, right = halo(left_out, right_out, "band")
    pred, pack = net(
        chans,
        rows,
        cols,
        n_band,
        (place, flags, feed, top, bot, left, right, own) + weights + (local_interp,),
    )
    pack = lax.all_to_all(pack, "band", split_axis=0, concat_axis=0, tiled=True)
    parts = lax.all_to_all(
        merge(asked, pack, n_tile), "tile", split_axis=0, concat_axis=0, tiled=True
    )
    coarse_grad, sums = share(
        parts, (1, per_band // n_tile) + coarse.shape[2:], n_tile * n_band
    )
    sums = lax.all_to_all(sums, ALL, split_axis=0, concat_axis=0, tiled=True)
    factor = 1.0 / math.sqrt(cells * n_tile * n_band)
    grad_in, grad_one, grad_two, grad_out = final(
        sums, n_band, width, w_conv1.shape, w_in.shape[1], chans, factor
    )
    return (pred, coarse_grad, grad_in.T, grad_one, grad_two, grad_out)


def solution(mesh):
    placed = (
        P(None, "tile", "band"),
        P(None, "tile", "band"),
        P("band", None, None, None),
        P(("tile", "band"), None),
        P(("tile", "band")),
        P("tile", "band", None, None, None),
        P(),
        P(),
        P(),
        P(),
    )
    return jax.shard_map(
        per_device,
        mesh=mesh,
        in_specs=placed,
        out_specs=(P(None, "tile", "band"), P("band", "tile", None, None), P(), P(), P(), P()),
        check_vma=False,
    )
```

```python
import functools
import math

import jax
import jax.numpy as jnp
import numpy as np
from jax import lax
from jax.experimental import pallas as pl
from jax.experimental.pallas import tpu as pltpu
from jax.sharding import PartitionSpec as P

MOST = 4
ALL = ("tile", "band")

FEED = 80
NOISY_AT = 48
GRAD_AT = 60
WIDE = 48
SUMS = 2432
OUT_AT = 80
HIGH = 96
CHUNK = 24
NT = (((1,), (1,)), ((), ()))


def f32dot(left, right):
    return jnp.dot(left, right, preferred_element_type=jnp.float32)


def vmem(mib):
    return pltpu.CompilerParams(vmem_limit_bytes=mib * 1024 * 1024)


def whole():
    return pl.BlockSpec(memory_space=pltpu.VMEM)


def scalars():
    return pl.BlockSpec(memory_space=pltpu.SMEM)


def plan_kernel(me_ref, band_ref, slot_ref, place_ref, near_ref, *wanted_refs):
    count = slot_ref.shape[0]
    n_band = len(wanted_refs)
    lane = lax.broadcasted_iota(jnp.int32, wanted_refs[0].shape, 1)
    wanted = [jnp.full(ref.shape, -1, jnp.int32) for ref in wanted_refs]
    for j in range(count):
        band = band_ref[j]
        rank = jnp.int32(0)
        for i in range(j):
            rank = rank + jnp.where(band_ref[i] == band, 1, 0)
        ahead = band - me_ref[0]
        ahead = jnp.where(ahead < 0, ahead + n_band, ahead)
        place_ref[j] = band * MOST + rank
        near_ref[j] = ahead * MOST + rank
        for k in range(n_band):
            spot = jnp.where(ahead == k, rank, -1)
            wanted[k] = jnp.where(lane == spot, slot_ref[j], wanted[k])
    for k in range(n_band):
        wanted_refs[k][...] = wanted[k]


def plan(me, bands, slots, n_band):
    return pl.pallas_call(
        plan_kernel,
        out_shape=(jax.ShapeDtypeStruct(slots.shape, jnp.int32),) * 2
        + (jax.ShapeDtypeStruct((8, 128), jnp.int32),) * n_band,
        in_specs=[scalars()] * 3,
        out_specs=(scalars(),) * 2 + (whole(),) * n_band,
    )(me, bands, slots)


def prep_kernel(
    noisy_ref,
    grad_ref,
    w_in_ref,
    w_out_ref,
    w_one_ref,
    w_two_ref,
    given_ref,
    first_ref,
    one_ref,
    one_back_ref,
    two_ref,
    two_back_ref,
    out_ref,
    cond_ref,
    small,
    noisy_wide,
    grad_wide,
):
    bf, f32 = jnp.bfloat16, jnp.float32
    chans, rows, _ = noisy_ref.shape
    coarse_ch = w_in_ref.shape[0] - chans
    ch = w_in_ref.shape[1]
    small[...] = jnp.zeros_like(small)
    w_in = w_in_ref[...].astype(f32)
    w_out = w_out_ref[...].astype(f32)
    small[0:coarse_ch, 0:ch] = w_in[0:coarse_ch]
    cond_ref[...] = small[0:WIDE, 0:ch].astype(bf)
    small[NOISY_AT : NOISY_AT + chans, 0:ch] = w_in[coarse_ch:]
    small[GRAD_AT : GRAD_AT + chans, ch:] = w_out
    first_ref[...] = small[...].T[:, 0:FEED].astype(bf)
    out_ref[...] = jnp.concatenate([w_out, jnp.zeros((16 - chans, ch), f32)], axis=0).astype(bf)
    for source, straight, back in (
        (w_one_ref, one_ref, one_back_ref),
        (w_two_ref, two_ref, two_back_ref),
    ):
        for tap in range(9):
            lanes = slice(tap * ch, (tap + 1) * ch)
            straight[:, lanes] = source[tap // 3, tap % 3]
            back[:, lanes] = source[2 - tap // 3, 2 - tap % 3].T
    noisy_wide[...] = noisy_ref[...].astype(f32)
    grad_wide[...] = grad_ref[...].astype(f32)
    pad = jnp.zeros((FEED - NOISY_AT - 2 * chans, 128), f32)
    for r in range(rows):
        pieces = [noisy_wide[:, r, :], grad_wide[:, r, :], pad]
        given_ref[:, r * 128 : (r + 1) * 128] = jnp.concatenate(pieces, axis=0).astype(bf)


def prep(noisy, grad_pred, w_in, w_out, w_one, w_two):
    bf = jnp.bfloat16
    chans, rows, cols = noisy.shape
    ch = w_in.shape[0]
    square = jax.ShapeDtypeStruct((ch, 9 * ch), bf)
    return pl.pallas_call(
        prep_kernel,
        out_shape=(
            jax.ShapeDtypeStruct((FEED - NOISY_AT, rows * cols), bf),
            jax.ShapeDtypeStruct((2 * ch, FEED), bf),
            square,
            square,
            square,
            square,
            jax.ShapeDtypeStruct((16, ch), bf),
            jax.ShapeDtypeStruct((WIDE, ch), bf),
        ),
        in_specs=[whole()] * 6,
        out_specs=(whole(),) * 8,
        scratch_shapes=[
            pltpu.VMEM((128, 2 * ch), jnp.float32),
            pltpu.VMEM(noisy.shape, jnp.float32),
            pltpu.VMEM(noisy.shape, jnp.float32),
        ],
        compiler_params=vmem(56),
    )(noisy, grad_pred, w_in.T, w_out, w_one, w_two)


def serve_kernel(n_band, *refs):
    asked_refs, coarse_ref, out_refs = refs[:n_band], refs[n_band], refs[n_band + 1 :]
    for asked_ref, out_ref in zip(asked_refs, out_refs):
        for i in range(MOST):
            out_ref[i] = coarse_ref[jnp.maximum(asked_ref[0, i], 0)]


def serve(asked, coarse):
    n_band = len(asked)
    shape = jax.ShapeDtypeStruct((MOST,) + coarse.shape[1:], coarse.dtype)
    return pl.pallas_call(
        functools.partial(serve_kernel, n_band),
        out_shape=(shape,) * n_band,
        in_specs=[scalars()] * n_band + [whole()],
        out_specs=(whole(),) * n_band,
        compiler_params=vmem(4),
    )(*asked, coarse)


def feed_kernel(n_band, near_ref, *refs):
    arrived_refs = refs[:n_band]
    interp_ref, given_ref, hit_ref = refs[n_band : n_band + 3]
    feed_ref, first_ref, last_ref, edge_ref, arrived, picked = refs[n_band + 3 :]
    ch = arrived.shape[1]
    count, cells, n = interp_ref.shape
    lanes = hit_ref.shape[0]
    bf = jnp.bfloat16
    for k in range(n_band):
        arrived[k * MOST : (k + 1) * MOST] = arrived_refs[k][...]
    for j in range(count):
        picked[:, j * cells : (j + 1) * cells] = arrived[near_ref[j]]
    feed_ref[...] = jnp.zeros_like(feed_ref)
    feed_ref[NOISY_AT:, :] = given_ref[...]
    edge = jnp.zeros(edge_ref.shape, jnp.float32)
    for step in range(n // lanes):
        block = slice(step * lanes, (step + 1) * lanes)
        matrix = interp_ref[:, :, block].reshape(count * cells, lanes)
        feed_ref[0:ch, block] = f32dot(picked[...], matrix).astype(bf)
        piece = f32dot(feed_ref[:, block], hit_ref[...])
        edge = edge + pltpu.roll(piece, 2 + step * (lanes // 128), 1)
    edge_ref[...] = edge.astype(bf)
    first_ref[...] = feed_ref[:, 0:256]
    last_ref[...] = feed_ref[:, n - 256 :]


def stash_kernel(source_ref, out_ref):
    pltpu.sync_copy(source_ref, out_ref)


def stash(array):
    return pl.pallas_call(
        stash_kernel,
        out_shape=pltpu.VMEM(array.shape, array.dtype),
        in_specs=[pl.BlockSpec(memory_space=pltpu.HBM)],
        out_specs=whole(),
        compiler_params=vmem(4),
    )(pltpu.with_memory_space_constraint(array, pltpu.HBM))


def column_picks(lanes):
    hit = np.zeros((lanes, 256), np.float32)
    for k, col in enumerate((0, 1, 126, 127)):
        for r in range(lanes // 128):
            hit[r * 128 + col, k * 64 + r] = 1.0
    return jnp.asarray(hit, jnp.bfloat16)


def make_feed(near, arrived, interp, given, blocks=4):
    count, cells, n = interp.shape
    n_band = len(arrived)
    ch = arrived[0].shape[1]
    bf = jnp.bfloat16
    side = jax.ShapeDtypeStruct((FEED, 256), bf)
    return pl.pallas_call(
        functools.partial(feed_kernel, n_band),
        out_shape=(jax.ShapeDtypeStruct((FEED, n), bf), side, side, side),
        in_specs=[scalars()] + [whole()] * (n_band + 3),
        out_specs=(whole(),) * 4,
        scratch_shapes=[
            pltpu.VMEM((n_band * MOST, ch, cells), bf),
            pltpu.VMEM((ch, count * cells), bf),
        ],
        compiler_params=vmem(16),
    )(near, *arrived, interp, given, column_picks(n // blocks))


def strip_kernel(top_ref, bot_ref, edge_ref, left_ref, right_ref, own_ref):
    wide = jnp.concatenate([top_ref[...], bot_ref[...]], axis=1)
    at = lax.broadcasted_iota(jnp.int32, (512, 256), 0)
    lane = lax.broadcasted_iota(jnp.int32, (512, 256), 1)
    spot = jnp.bitwise_and(lane, 63)
    row = jnp.where(spot < 2, spot, jnp.where(jnp.logical_or(spot == 34, spot == 35), spot - 32, 8))
    kind = jnp.right_shift(lane, 6)
    col = kind + jnp.where(kind >= 2, 124, 0)
    hit = jnp.where(row * 128 + col == at, 1.0, 0.0).astype(jnp.bfloat16)
    edge = (edge_ref[...].astype(jnp.float32) + f32dot(wide, hit)).astype(jnp.bfloat16)
    left_ref[...] = edge[:, 0:128]
    right_ref[...] = edge[:, 128:256]
    own_ref[...] = jnp.concatenate([edge[:, 0:64], edge[:, 192:256]], axis=1)


def strips(top, bot, edge):
    shape = jax.ShapeDtypeStruct((FEED, 128), jnp.bfloat16)
    return pl.pallas_call(
        strip_kernel,
        out_shape=(shape,) * 3,
        in_specs=[whole()] * 3,
        out_specs=(whole(),) * 3,
        compiler_params=vmem(4),
    )(top, bot, edge)


def silu_parts(value):
    sig = jax.nn.sigmoid(value)
    return value * sig, sig * (1.0 + value * (1.0 - sig))


def net_kernel(
    place_ref,
    flag_ref,
    feed_ref,
    top_ref,
    bot_ref,
    left_ref,
    right_ref,
    own_ref,
    w_first_ref,
    w_one_ref,
    w_one_back_ref,
    w_two_ref,
    w_two_back_ref,
    w_out_ref,
    w_cond_ref,
    interp_ref,
    pred_ref,
    pack_ref,
    x_ref,
    a_zero_ref,
    d_two_ref,
    a_one_ref,
    d_one_ref,
    slope_ref,
    sum_one_ref,
    sum_two_ref,
    dcond_ref,
):
    rows = pred_ref.shape[1]
    tall = rows + 4
    ch = 128
    bf, f32 = jnp.bfloat16, jnp.float32
    lane = lax.broadcasted_iota(jnp.int32, (ch, 128), 1)
    at_left = lane == 0
    at_right = lane == 127

    def put(ref, row, value, edge, edge_row):
        lanes = slice(row * 128, (row + 1) * 128)
        value = value.astype(f32)
        left = pltpu.roll(edge, (128 - edge_row) % 128, 1)
        right = pltpu.roll(edge, 63 - edge_row, 1)
        ref[0:ch, lanes] = jnp.where(at_left, left, pltpu.roll(value, 1, 1)).astype(bf)
        ref[ch : 2 * ch, lanes] = value.astype(bf)
        ref[2 * ch :, lanes] = jnp.where(at_right, right, pltpu.roll(value, 127, 1)).astype(bf)

    def around(ref, row, count):
        return jnp.concatenate(
            [ref[:, (row + p) * 128 : (row + p + count) * 128] for p in range(3)], axis=0
        )

    left, right, own = left_ref[...], right_ref[...], own_ref[...]
    groups = (
        jnp.concatenate([left[:, 0:64], own[:, 64:128]], axis=1),
        jnp.concatenate([left[:, 64:128], right[:, 0:64]], axis=1),
        jnp.concatenate([own[:, 0:64], right[:, 64:128]], axis=1),
    )
    edge_x = jnp.concatenate(groups, axis=1)
    both = f32dot(w_first_ref[...], edge_x)
    edge_a = silu_parts(both[0:ch])[0].astype(bf).astype(f32)
    edge_d = both[ch:].astype(bf).astype(f32)

    def edge_taps(field):
        pieces = []
        for p in range(3):
            for q in range(3):
                part = field[:, q * 128 : (q + 1) * 128]
                pieces.append(part if p == 1 else pltpu.roll(part, (1 - p) % 128, 1))
        return jnp.concatenate(pieces, axis=0).astype(bf)

    spot = jnp.bitwise_and(lane, 63)
    edge_in = jnp.where(lane >= 64, flag_ref[3], flag_ref[2])
    edge_in = edge_in * jnp.where(spot == 1, flag_ref[0], 1.0)
    edge_in = edge_in * jnp.where(spot == rows + 2, flag_ref[1], 1.0)
    edge_act, edge_slope = silu_parts(f32dot(w_one_ref[...], edge_taps(edge_a)))
    edge_a_one = (edge_act * edge_in).astype(bf).astype(f32)
    edge_back = f32dot(w_two_back_ref[...], edge_taps(edge_d))
    edge_d_one = (edge_back * edge_slope * edge_in).astype(bf).astype(f32)
    edge_a = edge_a[:, 128:256]
    edge_d = edge_d[:, 128:256]

    x_ref[:, 0:256] = top_ref[...]
    x_ref[:, 256 : (rows + 2) * 128] = feed_ref[...]
    x_ref[:, (rows + 2) * 128 :] = bot_ref[...]
    for row in range(0, tall, 4):
        both = f32dot(w_first_ref[...], x_ref[:, row * 128 : (row + 4) * 128])
        act, slope = silu_parts(both[0:ch])
        slope_ref[:, row * 128 : (row + 4) * 128] = slope
        for k in range(4):
            lanes = slice(k * 128, (k + 1) * 128)
            put(a_zero_ref, row + k, act[:, lanes], edge_a, row + k)
            put(d_two_ref, row + k, both[ch:, lanes], edge_d, row + k)

    act, slope = silu_parts(f32dot(w_one_ref[...], around(a_zero_ref, 0, rows + 2)))
    back = f32dot(w_two_back_ref[...], around(d_two_ref, 0, rows + 2)) * slope
    for row in range(rows + 2):
        lanes = slice(row * 128, (row + 1) * 128)
        act_row, back_row = act[:, lanes], back[:, lanes]
        if row == 0:
            act_row, back_row = act_row * flag_ref[0], back_row * flag_ref[0]
        if row == rows + 1:
            act_row, back_row = act_row * flag_ref[1], back_row * flag_ref[1]
        put(a_one_ref, row, act_row, edge_a_one, row + 1)
        put(d_one_ref, row, back_row, edge_d_one, row + 1)

    mine = slice(256, (rows + 2) * 128)
    x = x_ref[:, mine]
    d_two = d_two_ref[ch : 2 * ch, mine]
    cols_one = around(a_one_ref, 0, rows)
    z_two = f32dot(w_two_ref[...], cols_one)
    a_two = (a_zero_ref[ch : 2 * ch, mine].astype(f32) + z_two).astype(bf)
    pred = f32dot(w_out_ref[...], a_two)
    for k in range(rows):
        pred_ref[:, k, :] = pred[0 : pred_ref.shape[0], k * 128 : (k + 1) * 128]
    sum_out = nt_dot(a_two, x[NOISY_AT:, :])
    sum_two_ref[...] = nt_dot(d_two, cols_one)
    back = f32dot(w_one_back_ref[...], around(d_one_ref, 0, rows))
    d_zero = ((back + d_two.astype(f32)) * slope_ref[:, mine]).astype(bf)
    sum_in = nt_dot(d_zero, x)
    dcond_ref[...] = f32dot(w_cond_ref[...], d_zero).astype(bf)
    d_one = d_one_ref[ch : 2 * ch, 128 : (rows + 1) * 128]
    sum_one_ref[...] = nt_dot(d_one, around(a_zero_ref, 1, rows))

    bands = pack_ref.shape[0]
    share_rows = SUMS // bands

    def store(first, value):
        done = 0
        while done < value.shape[0]:
            band, spot = divmod(first + done, share_rows)
            count = min(value.shape[0] - done, share_rows - spot)
            pack_ref[band, spot : spot + count, :] = value[done : done + count, :]
            done += count

    for tap in range(9):
        lanes = slice(tap * 128, (tap + 1) * 128)
        store(tap * ch, sum_two_ref[:, lanes].astype(bf))
        store((9 + tap) * ch, sum_one_ref[:, lanes].astype(bf))
    pad = jnp.zeros((ch, 128 - OUT_AT - (FEED - NOISY_AT)), f32)
    store(18 * ch, jnp.concatenate([sum_in, sum_out, pad], axis=1).astype(bf))
    for band in range(bands):
        pack_ref[band, share_rows:, :] = jnp.zeros((MOST * WIDE, 128), bf)
    count, cells, n = interp_ref.shape
    blocks = nt_dot(dcond_ref[...], interp_ref[...].reshape(count * cells, n)).astype(bf)
    for j in range(count):
        place = place_ref[j]
        spot = share_rows + jnp.bitwise_and(place, MOST - 1) * WIDE
        pack_ref[jnp.right_shift(place, 2), pl.ds(pl.multiple_of(spot, 16), WIDE), :] = blocks[
            :, j * cells : (j + 1) * cells
        ]


def nt_dot(left, right):
    return lax.dot_general(left, right, NT, preferred_element_type=jnp.float32)


def net(chans, rows, cols, n_band, args):
    ch = 128
    bf, f32 = jnp.bfloat16, jnp.float32
    tall = (rows + 4) * cols
    inner = (rows + 2) * cols
    return pl.pallas_call(
        net_kernel,
        out_shape=(
            jax.ShapeDtypeStruct((chans, rows, cols), f32),
            jax.ShapeDtypeStruct((n_band, SUMS // n_band + MOST * WIDE, 128), bf),
        ),
        in_specs=[scalars(), scalars()]
        + [whole()] * (len(args) - 2),
        out_specs=(whole(),) * 2,
        scratch_shapes=[
            pltpu.VMEM((FEED, tall), bf),
            pltpu.VMEM((3 * ch, tall), bf),
            pltpu.VMEM((3 * ch, tall), bf),
            pltpu.VMEM((3 * ch, inner), bf),
            pltpu.VMEM((3 * ch, inner), bf),
            pltpu.VMEM((ch, tall), f32),
            pltpu.VMEM((ch, 9 * ch), f32),
            pltpu.VMEM((ch, 9 * ch), f32),
            pltpu.VMEM((WIDE, rows * cols), bf),
        ],
        compiler_params=vmem(36),
    )(*args)


def merge_kernel(ch, n_band, me_ref, *refs):
    asked_refs = refs[:n_band]
    parts_ref, out_ref, total, weights = refs[n_band:]
    bands = n_band
    dests = out_ref.shape[0]
    share_rows = weights.shape[0]
    f32 = jnp.float32
    total[...] = jnp.zeros_like(total)
    whole_sum = parts_ref[0, 0:share_rows, :].astype(f32)
    for band in range(1, bands):
        whole_sum = whole_sum + parts_ref[band, 0:share_rows, :].astype(f32)
    weights[...] = whole_sum
    each = share_rows // dests
    for dest in range(dests):
        total[dest, 2 * ch : 2 * ch + each, :] = weights[dest * each : (dest + 1) * each, :]
    for i in range(bands * MOST):
        band = me_ref[0] - i // MOST
        band = jnp.where(band < 0, band + bands, band)
        slot = asked_refs[i // MOST][0, i % MOST]
        start = share_rows + (i % MOST) * WIDE
        block = parts_ref[band, start : start + WIDE, :].astype(f32)[0:ch]
        odd = jnp.bitwise_and(slot, 1)

        @pl.when(jnp.logical_and(slot >= 0, odd == 0))
        def _(slot=slot, block=block):
            total[jnp.right_shift(slot, 1), 0:ch, :] += block

        @pl.when(jnp.logical_and(slot >= 0, odd == 1))
        def _(slot=slot, block=block):
            total[jnp.right_shift(slot, 1), ch : 2 * ch, :] += block

    out_ref[...] = total[...].astype(jnp.bfloat16)


def merge(me, asked, parts, dests, ch):
    n_band = len(asked)
    return pl.pallas_call(
        functools.partial(merge_kernel, ch, n_band),
        out_shape=jax.ShapeDtypeStruct((dests, HIGH, 128), jnp.bfloat16),
        in_specs=[scalars()] * (n_band + 1) + [whole()],
        out_specs=whole(),
        scratch_shapes=[
            pltpu.VMEM((dests, HIGH, 128), jnp.float32),
            pltpu.VMEM((SUMS // parts.shape[0], 128), jnp.float32),
        ],
        compiler_params=vmem(12),
    )(me, *asked, parts)


def share_kernel(parts_ref, block_ref, out_ref, total):
    value = parts_ref[0].astype(jnp.float32)
    for i in range(1, parts_ref.shape[0]):
        value = value + parts_ref[i].astype(jnp.float32)
    total[...] = value
    ch = block_ref.shape[2]
    for k in range(block_ref.shape[1]):
        block_ref[0, k] = total[k * ch : (k + 1) * ch, :]
    rest = block_ref.shape[1] * ch
    chunk = value[rest:].astype(jnp.bfloat16)
    chunk = jnp.concatenate([chunk, jnp.zeros((CHUNK - chunk.shape[0], 128), jnp.bfloat16)], axis=0)
    out_ref[...] = jnp.broadcast_to(chunk[None], out_ref.shape)


def share(parts, block_shape, devices):
    return pl.pallas_call(
        share_kernel,
        out_shape=(
            jax.ShapeDtypeStruct(block_shape, jnp.float32),
            jax.ShapeDtypeStruct((devices, CHUNK, 128), jnp.bfloat16),
        ),
        in_specs=[whole()],
        out_specs=(whole(), whole()),
        scratch_shapes=[pltpu.VMEM((HIGH, 128), jnp.float32)],
        compiler_params=vmem(8),
    )(parts)


def final_kernel(factor, n_band, parts_ref, in_ref, one_ref, two_ref, out_ref, total):
    ch = in_ref.shape[1]
    side = two_ref.shape[0]
    devices = parts_ref.shape[0]
    each = SUMS // devices
    for device in range(devices):
        tile, band = divmod(device, n_band)
        first = (band * (devices // n_band) + tile) * each
        total[first : first + each, :] = parts_ref[device].astype(jnp.float32)[0:each] * factor
    for tap in range(9):
        two_ref[tap // side, tap % side] = total[tap * ch : (tap + 1) * ch, :]
        one_ref[tap // side, tap % side] = total[(9 + tap) * ch : (10 + tap) * ch, :]
    last = total[18 * ch : 19 * ch, :]
    chans = out_ref.shape[0]
    coarse_ch = in_ref.shape[0] - chans
    flipped = last.T
    in_ref[0:coarse_ch, :] = flipped[0:coarse_ch, :]
    in_ref[coarse_ch:, :] = flipped[NOISY_AT : NOISY_AT + chans, :]
    start = OUT_AT + GRAD_AT - NOISY_AT
    out_ref[...] = flipped[start : start + chans, :]


def final(parts, n_band, width, taps, inner, chans, factor):
    f32 = jnp.float32
    return pl.pallas_call(
        functools.partial(final_kernel, factor, n_band),
        out_shape=(
            jax.ShapeDtypeStruct((inner, width), f32),
            jax.ShapeDtypeStruct(taps, f32),
            jax.ShapeDtypeStruct(taps, f32),
            jax.ShapeDtypeStruct((chans, width), f32),
        ),
        in_specs=[whole()],
        out_specs=(whole(),) * 4,
        scratch_shapes=[pltpu.VMEM((SUMS, 128), f32)],
        compiler_params=vmem(12),
    )(parts)


def halo(first, last, axis):
    count = lax.axis_size(axis)
    up = [(i, i + 1) for i in range(count - 1)]
    down = [(i + 1, i) for i in range(count - 1)]
    return lax.ppermute(last, axis, up), lax.ppermute(first, axis, down)


def ahead(parts, axis, way):
    count = lax.axis_size(axis)
    moved = [parts[0]]
    for k in range(1, count):
        pairs = [(i, (i + k * way) % count) for i in range(count)]
        moved.append(lax.ppermute(parts[k], axis, pairs))
    return moved


def per_device(
    noisy, grad_pred, coarse, margin_band, margin_slot, interp, w_in, w_conv1, w_conv2, w_out
):
    width = w_in.shape[0]
    chans, rows, cols = noisy.shape
    cells = rows * cols
    coarse_ch = coarse.shape[2]
    per_band = coarse.shape[1]
    n_band = lax.axis_size("band")
    n_tile = lax.axis_size("tile")
    local_interp = interp[0, 0]

    tile, band = lax.axis_index("tile"), lax.axis_index("band")
    flags = jnp.stack([tile > 0, tile < n_tile - 1, band > 0, band < n_band - 1])
    flags = flags.astype(jnp.float32)
    me = band.reshape(1)
    place, near, *wanted = plan(me, margin_band.reshape(-1), margin_slot, n_band)
    asked = ahead(wanted, "band", 1)
    prepared = prep(noisy, grad_pred, w_in, w_out, w_conv1, w_conv2)
    asked, prepared, flags, late = lax.optimization_barrier(
        (asked, prepared, flags, local_interp)
    )
    stashed = pltpu.with_memory_space_constraint(stash(late), pltpu.VMEM)
    given, weights = prepared[0], tuple(prepared[1:])
    arrived = ahead(serve(asked, coarse[0]), "band", -1)
    feed, first, last, edge = make_feed(near, arrived, stashed, given)
    top, bot = halo(first, last, "tile")
    left_out, right_out, own = strips(top, bot, edge)
    left, right = halo(left_out, right_out, "band")
    pred, pack = net(
        chans,
        rows,
        cols,
        n_band,
        (place, flags, feed, top, bot, left, right, own) + weights + (stashed,),
    )
    pack = lax.all_to_all(pack, "band", split_axis=0, concat_axis=0, tiled=True)
    parts = lax.all_to_all(
        merge(me, asked, pack, n_tile, coarse_ch), "tile", split_axis=0, concat_axis=0, tiled=True
    )
    coarse_grad, sums = share(
        parts, (1, per_band // n_tile) + coarse.shape[2:], n_tile * n_band
    )
    sums = lax.all_to_all(sums, ALL, split_axis=0, concat_axis=0, tiled=True)
    factor = 1.0 / math.sqrt(cells * n_tile * n_band)
    grad_in, grad_one, grad_two, grad_out = final(
        sums, n_band, width, w_conv1.shape, w_in.shape[1], chans, factor
    )
    return (pred, coarse_grad, grad_in.T, grad_one, grad_two, grad_out)


def solution(mesh):
    placed = (
        P(None, "tile", "band"),
        P(None, "tile", "band"),
        P("band", None, None, None),
        P(("tile", "band"), None),
        P(("tile", "band")),
        P("tile", "band", None, None, None),
        P(),
        P(),
        P(),
        P(),
    )
    return jax.shard_map(
        per_device,
        mesh=mesh,
        in_specs=placed,
        out_specs=(P(None, "tile", "band"), P("band", "tile", None, None), P(), P(), P(), P()),
        check_vma=False,
    )
```

```python
import functools
import math

import jax
import jax.numpy as jnp
import numpy as np
from jax import lax
from jax.experimental import pallas as pl
from jax.experimental.pallas import tpu as pltpu
from jax.sharding import PartitionSpec as P

MOST = 4
ALL = ("tile", "band")

FEED = 80
NOISY_AT = 48
GRAD_AT = 60
WIDE = 48
SUMS = 2432
OUT_AT = 80
HIGH = 96
CHUNK = 24
NT = (((1,), (1,)), ((), ()))


def f32dot(left, right):
    return jnp.dot(left, right, preferred_element_type=jnp.float32)


def vmem(mib):
    return pltpu.CompilerParams(vmem_limit_bytes=mib * 1024 * 1024)


def whole():
    return pl.BlockSpec(memory_space=pltpu.VMEM)


def scalars():
    return pl.BlockSpec(memory_space=pltpu.SMEM)


def plan_kernel(me_ref, band_ref, slot_ref, place_ref, near_ref, *wanted_refs):
    count = slot_ref.shape[0]
    n_band = len(wanted_refs)
    lane = lax.broadcasted_iota(jnp.int32, wanted_refs[0].shape, 1)
    wanted = [jnp.full(ref.shape, -1, jnp.int32) for ref in wanted_refs]
    for j in range(count):
        band = band_ref[j]
        rank = jnp.int32(0)
        for i in range(j):
            rank = rank + jnp.where(band_ref[i] == band, 1, 0)
        ahead = band - me_ref[0]
        ahead = jnp.where(ahead < 0, ahead + n_band, ahead)
        place_ref[j] = band * MOST + rank
        near_ref[j] = ahead * MOST + rank
        for k in range(n_band):
            spot = jnp.where(ahead == k, rank, -1)
            wanted[k] = jnp.where(lane == spot, slot_ref[j], wanted[k])
    for k in range(n_band):
        wanted_refs[k][...] = wanted[k]


def plan(me, bands, slots, n_band):
    return pl.pallas_call(
        plan_kernel,
        out_shape=(jax.ShapeDtypeStruct(slots.shape, jnp.int32),) * 2
        + (jax.ShapeDtypeStruct((8, 128), jnp.int32),) * n_band,
        in_specs=[scalars()] * 3,
        out_specs=(scalars(),) * 2 + (whole(),) * n_band,
    )(me, bands, slots)


def given_kernel(noisy_ref, grad_ref, given_ref, noisy_wide, grad_wide):
    bf, f32 = jnp.bfloat16, jnp.float32
    chans, rows, _ = noisy_ref.shape
    noisy_wide[...] = noisy_ref[...].astype(f32)
    grad_wide[...] = grad_ref[...].astype(f32)
    pad = jnp.zeros((FEED - NOISY_AT - 2 * chans, 128), f32)
    for r in range(rows):
        pieces = [noisy_wide[:, r, :], grad_wide[:, r, :], pad]
        given_ref[:, r * 128 : (r + 1) * 128] = jnp.concatenate(pieces, axis=0).astype(bf)


def make_given(noisy, grad_pred):
    _, rows, cols = noisy.shape
    return pl.pallas_call(
        given_kernel,
        out_shape=jax.ShapeDtypeStruct((FEED - NOISY_AT, rows * cols), jnp.bfloat16),
        in_specs=[whole()] * 2,
        out_specs=whole(),
        scratch_shapes=[
            pltpu.VMEM(noisy.shape, jnp.float32),
            pltpu.VMEM(noisy.shape, jnp.float32),
        ],
        compiler_params=vmem(56),
    )(noisy, grad_pred)


def prep_kernel(
    w_in_ref,
    w_out_ref,
    w_one_ref,
    w_two_ref,
    first_ref,
    one_ref,
    one_back_ref,
    two_ref,
    two_back_ref,
    out_ref,
    cond_ref,
    small,
):
    bf, f32 = jnp.bfloat16, jnp.float32
    chans, ch = w_out_ref.shape
    coarse_ch = w_in_ref.shape[0] - chans
    small[...] = jnp.zeros_like(small)
    w_in = w_in_ref[...].astype(f32)
    w_out = w_out_ref[...].astype(f32)
    small[0:coarse_ch, 0:ch] = w_in[0:coarse_ch]
    cond_ref[...] = small[0:WIDE, 0:ch].astype(bf)
    small[NOISY_AT : NOISY_AT + chans, 0:ch] = w_in[coarse_ch:]
    small[GRAD_AT : GRAD_AT + chans, ch:] = w_out
    first_ref[...] = small[...].T[:, 0:FEED].astype(bf)
    out_ref[...] = jnp.concatenate([w_out, jnp.zeros((16 - chans, ch), f32)], axis=0).astype(bf)
    for source, straight, back in (
        (w_one_ref, one_ref, one_back_ref),
        (w_two_ref, two_ref, two_back_ref),
    ):
        for tap in range(9):
            lanes = slice(tap * ch, (tap + 1) * ch)
            straight[:, lanes] = source[tap // 3, tap % 3]
            back[:, lanes] = source[2 - tap // 3, 2 - tap % 3].T


def prep(w_in, w_out, w_one, w_two):
    bf = jnp.bfloat16
    ch = w_in.shape[0]
    square = jax.ShapeDtypeStruct((ch, 9 * ch), bf)
    return pl.pallas_call(
        prep_kernel,
        out_shape=(
            jax.ShapeDtypeStruct((2 * ch, FEED), bf),
            square,
            square,
            square,
            square,
            jax.ShapeDtypeStruct((16, ch), bf),
            jax.ShapeDtypeStruct((WIDE, ch), bf),
        ),
        in_specs=[whole()] * 4,
        out_specs=(whole(),) * 7,
        scratch_shapes=[pltpu.VMEM((128, 2 * ch), jnp.float32)],
        compiler_params=vmem(8),
    )(w_in.T, w_out, w_one, w_two)


def serve_kernel(n_band, *refs):
    asked_refs, coarse_ref, out_refs = refs[:n_band], refs[n_band], refs[n_band + 1 :]
    for asked_ref, out_ref in zip(asked_refs, out_refs):
        for i in range(MOST):
            out_ref[i] = coarse_ref[jnp.maximum(asked_ref[0, i], 0)]


def serve(asked, coarse):
    n_band = len(asked)
    shape = jax.ShapeDtypeStruct((MOST,) + coarse.shape[1:], coarse.dtype)
    return pl.pallas_call(
        functools.partial(serve_kernel, n_band),
        out_shape=(shape,) * n_band,
        in_specs=[scalars()] * n_band + [whole()],
        out_specs=(whole(),) * n_band,
        compiler_params=vmem(4),
    )(*asked, coarse)


def feed_kernel(n_band, near_ref, *refs):
    arrived_refs = refs[:n_band]
    interp_ref, given_ref, hit_ref = refs[n_band : n_band + 3]
    feed_ref, first_ref, last_ref, edge_ref, arrived, picked = refs[n_band + 3 :]
    ch = arrived.shape[1]
    count, cells, n = interp_ref.shape
    lanes = hit_ref.shape[0]
    bf = jnp.bfloat16
    for k in range(n_band):
        arrived[k * MOST : (k + 1) * MOST] = arrived_refs[k][...]
    for j in range(count):
        picked[:, j * cells : (j + 1) * cells] = arrived[near_ref[j]]
    feed_ref[...] = jnp.zeros_like(feed_ref)
    feed_ref[NOISY_AT:, :] = given_ref[...]
    edge = jnp.zeros(edge_ref.shape, jnp.float32)
    for step in range(n // lanes):
        block = slice(step * lanes, (step + 1) * lanes)
        matrix = interp_ref[:, :, block].reshape(count * cells, lanes)
        feed_ref[0:ch, block] = f32dot(picked[...], matrix).astype(bf)
        piece = f32dot(feed_ref[:, block], hit_ref[...])
        edge = edge + pltpu.roll(piece, 2 + step * (lanes // 128), 1)
    edge_ref[...] = edge.astype(bf)
    first_ref[...] = feed_ref[:, 0:256]
    last_ref[...] = feed_ref[:, n - 256 :]


def stash_kernel(source_ref, out_ref):
    pltpu.sync_copy(source_ref, out_ref)


def stash(array):
    return pl.pallas_call(
        stash_kernel,
        out_shape=pltpu.VMEM(array.shape, array.dtype),
        in_specs=[pl.BlockSpec(memory_space=pltpu.HBM)],
        out_specs=whole(),
        compiler_params=vmem(4),
    )(pltpu.with_memory_space_constraint(array, pltpu.HBM))


def column_picks(lanes):
    hit = np.zeros((lanes, 256), np.float32)
    for k, col in enumerate((0, 1, 126, 127)):
        for r in range(lanes // 128):
            hit[r * 128 + col, k * 64 + r] = 1.0
    return jnp.asarray(hit, jnp.bfloat16)


def make_feed(near, arrived, interp, given, blocks=4):
    count, cells, n = interp.shape
    n_band = len(arrived)
    ch = arrived[0].shape[1]
    bf = jnp.bfloat16
    side = jax.ShapeDtypeStruct((FEED, 256), bf)
    return pl.pallas_call(
        functools.partial(feed_kernel, n_band),
        out_shape=(jax.ShapeDtypeStruct((FEED, n), bf), side, side, side),
        in_specs=[scalars()] + [whole()] * (n_band + 3),
        out_specs=(whole(),) * 4,
        scratch_shapes=[
            pltpu.VMEM((n_band * MOST, ch, cells), bf),
            pltpu.VMEM((ch, count * cells), bf),
        ],
        compiler_params=vmem(16),
    )(near, *arrived, interp, given, column_picks(n // blocks))


def strip_kernel(top_ref, bot_ref, edge_ref, left_ref, right_ref, own_ref):
    wide = jnp.concatenate([top_ref[...], bot_ref[...]], axis=1)
    at = lax.broadcasted_iota(jnp.int32, (512, 256), 0)
    lane = lax.broadcasted_iota(jnp.int32, (512, 256), 1)
    spot = jnp.bitwise_and(lane, 63)
    row = jnp.where(spot < 2, spot, jnp.where(jnp.logical_or(spot == 34, spot == 35), spot - 32, 8))
    kind = jnp.right_shift(lane, 6)
    col = kind + jnp.where(kind >= 2, 124, 0)
    hit = jnp.where(row * 128 + col == at, 1.0, 0.0).astype(jnp.bfloat16)
    edge = (edge_ref[...].astype(jnp.float32) + f32dot(wide, hit)).astype(jnp.bfloat16)
    left_ref[...] = edge[:, 0:128]
    right_ref[...] = edge[:, 128:256]
    own_ref[...] = jnp.concatenate([edge[:, 0:64], edge[:, 192:256]], axis=1)


def strips(top, bot, edge):
    shape = jax.ShapeDtypeStruct((FEED, 128), jnp.bfloat16)
    return pl.pallas_call(
        strip_kernel,
        out_shape=(shape,) * 3,
        in_specs=[whole()] * 3,
        out_specs=(whole(),) * 3,
        compiler_params=vmem(4),
    )(top, bot, edge)


def silu_parts(value):
    sig = jax.nn.sigmoid(value)
    return value * sig, sig * (1.0 + value * (1.0 - sig))


def net_kernel(
    place_ref,
    flag_ref,
    feed_ref,
    top_ref,
    bot_ref,
    left_ref,
    right_ref,
    own_ref,
    w_first_ref,
    w_one_ref,
    w_one_back_ref,
    w_two_ref,
    w_two_back_ref,
    w_out_ref,
    w_cond_ref,
    interp_ref,
    pred_ref,
    pack_ref,
    x_ref,
    a_zero_ref,
    d_two_ref,
    a_one_ref,
    d_one_ref,
    slope_ref,
    sum_one_ref,
    sum_two_ref,
    dcond_ref,
):
    rows = pred_ref.shape[1]
    tall = rows + 4
    ch = 128
    bf, f32 = jnp.bfloat16, jnp.float32
    lane = lax.broadcasted_iota(jnp.int32, (ch, 128), 1)
    at_left = lane == 0
    at_right = lane == 127

    def put(ref, row, value, edge, edge_row):
        lanes = slice(row * 128, (row + 1) * 128)
        value = value.astype(f32)
        left = pltpu.roll(edge, (128 - edge_row) % 128, 1)
        right = pltpu.roll(edge, 63 - edge_row, 1)
        ref[0:ch, lanes] = jnp.where(at_left, left, pltpu.roll(value, 1, 1)).astype(bf)
        ref[ch : 2 * ch, lanes] = value.astype(bf)
        ref[2 * ch :, lanes] = jnp.where(at_right, right, pltpu.roll(value, 127, 1)).astype(bf)

    def around(ref, row, count):
        return jnp.concatenate(
            [ref[:, (row + p) * 128 : (row + p + count) * 128] for p in range(3)], axis=0
        )

    left, right, own = left_ref[...], right_ref[...], own_ref[...]
    groups = (
        jnp.concatenate([left[:, 0:64], own[:, 64:128]], axis=1),
        jnp.concatenate([left[:, 64:128], right[:, 0:64]], axis=1),
        jnp.concatenate([own[:, 0:64], right[:, 64:128]], axis=1),
    )
    edge_x = jnp.concatenate(groups, axis=1)
    both = f32dot(w_first_ref[...], edge_x)
    edge_a = silu_parts(both[0:ch])[0].astype(bf).astype(f32)
    edge_d = both[ch:].astype(bf).astype(f32)

    def edge_taps(field):
        pieces = []
        for p in range(3):
            for q in range(3):
                part = field[:, q * 128 : (q + 1) * 128]
                pieces.append(part if p == 1 else pltpu.roll(part, (1 - p) % 128, 1))
        return jnp.concatenate(pieces, axis=0).astype(bf)

    spot = jnp.bitwise_and(lane, 63)
    edge_in = jnp.where(lane >= 64, flag_ref[3], flag_ref[2])
    edge_in = edge_in * jnp.where(spot == 1, flag_ref[0], 1.0)
    edge_in = edge_in * jnp.where(spot == rows + 2, flag_ref[1], 1.0)
    edge_act, edge_slope = silu_parts(f32dot(w_one_ref[...], edge_taps(edge_a)))
    edge_a_one = (edge_act * edge_in).astype(bf).astype(f32)
    edge_back = f32dot(w_two_back_ref[...], edge_taps(edge_d))
    edge_d_one = (edge_back * edge_slope * edge_in).astype(bf).astype(f32)
    edge_a = edge_a[:, 128:256]
    edge_d = edge_d[:, 128:256]

    x_ref[:, 0:256] = top_ref[...]
    x_ref[:, 256 : (rows + 2) * 128] = feed_ref[...]
    x_ref[:, (rows + 2) * 128 :] = bot_ref[...]
    for row in range(0, tall, 4):
        both = f32dot(w_first_ref[...], x_ref[:, row * 128 : (row + 4) * 128])
        act, slope = silu_parts(both[0:ch])
        slope_ref[:, row * 128 : (row + 4) * 128] = slope
        for k in range(4):
            lanes = slice(k * 128, (k + 1) * 128)
            put(a_zero_ref, row + k, act[:, lanes], edge_a, row + k)
            put(d_two_ref, row + k, both[ch:, lanes], edge_d, row + k)

    act, slope = silu_parts(f32dot(w_one_ref[...], around(a_zero_ref, 0, rows + 2)))
    back = f32dot(w_two_back_ref[...], around(d_two_ref, 0, rows + 2)) * slope
    for row in range(rows + 2):
        lanes = slice(row * 128, (row + 1) * 128)
        act_row, back_row = act[:, lanes], back[:, lanes]
        if row == 0:
            act_row, back_row = act_row * flag_ref[0], back_row * flag_ref[0]
        if row == rows + 1:
            act_row, back_row = act_row * flag_ref[1], back_row * flag_ref[1]
        put(a_one_ref, row, act_row, edge_a_one, row + 1)
        put(d_one_ref, row, back_row, edge_d_one, row + 1)

    mine = slice(256, (rows + 2) * 128)
    x = x_ref[:, mine]
    d_two = d_two_ref[ch : 2 * ch, mine]
    cols_one = around(a_one_ref, 0, rows)
    z_two = f32dot(w_two_ref[...], cols_one)
    a_two = (a_zero_ref[ch : 2 * ch, mine].astype(f32) + z_two).astype(bf)
    pred = f32dot(w_out_ref[...], a_two)
    for k in range(rows):
        pred_ref[:, k, :] = pred[0 : pred_ref.shape[0], k * 128 : (k + 1) * 128]
    sum_out = nt_dot(a_two, x[NOISY_AT:, :])
    sum_two_ref[...] = nt_dot(d_two, cols_one)
    back = f32dot(w_one_back_ref[...], around(d_one_ref, 0, rows))
    d_zero = ((back + d_two.astype(f32)) * slope_ref[:, mine]).astype(bf)
    sum_in = nt_dot(d_zero, x)
    dcond_ref[...] = f32dot(w_cond_ref[...], d_zero).astype(bf)
    d_one = d_one_ref[ch : 2 * ch, 128 : (rows + 1) * 128]
    sum_one_ref[...] = nt_dot(d_one, around(a_zero_ref, 1, rows))

    bands = pack_ref.shape[0]
    share_rows = SUMS // bands

    def store(first, value):
        done = 0
        while done < value.shape[0]:
            band, spot = divmod(first + done, share_rows)
            count = min(value.shape[0] - done, share_rows - spot)
            pack_ref[band, spot : spot + count, :] = value[done : done + count, :]
            done += count

    for tap in range(9):
        lanes = slice(tap * 128, (tap + 1) * 128)
        store(tap * ch, sum_two_ref[:, lanes].astype(bf))
        store((9 + tap) * ch, sum_one_ref[:, lanes].astype(bf))
    pad = jnp.zeros((ch, 128 - OUT_AT - (FEED - NOISY_AT)), f32)
    store(18 * ch, jnp.concatenate([sum_in, sum_out, pad], axis=1).astype(bf))
    for band in range(bands):
        pack_ref[band, share_rows:, :] = jnp.zeros((MOST * WIDE, 128), bf)
    count, cells, n = interp_ref.shape
    blocks = nt_dot(dcond_ref[...], interp_ref[...].reshape(count * cells, n)).astype(bf)
    for j in range(count):
        place = place_ref[j]
        spot = share_rows + jnp.bitwise_and(place, MOST - 1) * WIDE
        pack_ref[jnp.right_shift(place, 2), pl.ds(pl.multiple_of(spot, 16), WIDE), :] = blocks[
            :, j * cells : (j + 1) * cells
        ]


def nt_dot(left, right):
    return lax.dot_general(left, right, NT, preferred_element_type=jnp.float32)


def net(chans, rows, cols, n_band, args):
    ch = 128
    bf, f32 = jnp.bfloat16, jnp.float32
    tall = (rows + 4) * cols
    inner = (rows + 2) * cols
    return pl.pallas_call(
        net_kernel,
        out_shape=(
            jax.ShapeDtypeStruct((chans, rows, cols), f32),
            jax.ShapeDtypeStruct((n_band, SUMS // n_band + MOST * WIDE, 128), bf),
        ),
        in_specs=[scalars(), scalars()]
        + [whole()] * (len(args) - 2),
        out_specs=(whole(),) * 2,
        scratch_shapes=[
            pltpu.VMEM((FEED, tall), bf),
            pltpu.VMEM((3 * ch, tall), bf),
            pltpu.VMEM((3 * ch, tall), bf),
            pltpu.VMEM((3 * ch, inner), bf),
            pltpu.VMEM((3 * ch, inner), bf),
            pltpu.VMEM((ch, tall), f32),
            pltpu.VMEM((ch, 9 * ch), f32),
            pltpu.VMEM((ch, 9 * ch), f32),
            pltpu.VMEM((WIDE, rows * cols), bf),
        ],
        compiler_params=vmem(36),
    )(*args)


def merge_kernel(ch, n_band, me_ref, *refs):
    asked_refs = refs[:n_band]
    parts_ref, out_ref, total, weights = refs[n_band:]
    bands = n_band
    dests = out_ref.shape[0]
    share_rows = weights.shape[0]
    f32 = jnp.float32
    total[...] = jnp.zeros_like(total)
    whole_sum = parts_ref[0, 0:share_rows, :].astype(f32)
    for band in range(1, bands):
        whole_sum = whole_sum + parts_ref[band, 0:share_rows, :].astype(f32)
    weights[...] = whole_sum
    each = share_rows // dests
    for dest in range(dests):
        total[dest, 2 * ch : 2 * ch + each, :] = weights[dest * each : (dest + 1) * each, :]
    for i in range(bands * MOST):
        band = me_ref[0] - i // MOST
        band = jnp.where(band < 0, band + bands, band)
        slot = asked_refs[i // MOST][0, i % MOST]
        start = share_rows + (i % MOST) * WIDE
        block = parts_ref[band, start : start + WIDE, :].astype(f32)[0:ch]
        odd = jnp.bitwise_and(slot, 1)

        @pl.when(jnp.logical_and(slot >= 0, odd == 0))
        def _(slot=slot, block=block):
            total[jnp.right_shift(slot, 1), 0:ch, :] += block

        @pl.when(jnp.logical_and(slot >= 0, odd == 1))
        def _(slot=slot, block=block):
            total[jnp.right_shift(slot, 1), ch : 2 * ch, :] += block

    out_ref[...] = total[...].astype(jnp.bfloat16)


def merge(me, asked, parts, dests, ch):
    n_band = len(asked)
    return pl.pallas_call(
        functools.partial(merge_kernel, ch, n_band),
        out_shape=jax.ShapeDtypeStruct((dests, HIGH, 128), jnp.bfloat16),
        in_specs=[scalars()] * (n_band + 1) + [whole()],
        out_specs=whole(),
        scratch_shapes=[
            pltpu.VMEM((dests, HIGH, 128), jnp.float32),
            pltpu.VMEM((SUMS // parts.shape[0], 128), jnp.float32),
        ],
        compiler_params=vmem(12),
    )(me, *asked, parts)


def share_kernel(parts_ref, block_ref, out_ref, total):
    value = parts_ref[0].astype(jnp.float32)
    for i in range(1, parts_ref.shape[0]):
        value = value + parts_ref[i].astype(jnp.float32)
    total[...] = value
    ch = block_ref.shape[2]
    for k in range(block_ref.shape[1]):
        block_ref[0, k] = total[k * ch : (k + 1) * ch, :]
    rest = block_ref.shape[1] * ch
    chunk = value[rest:].astype(jnp.bfloat16)
    chunk = jnp.concatenate([chunk, jnp.zeros((CHUNK - chunk.shape[0], 128), jnp.bfloat16)], axis=0)
    out_ref[...] = jnp.broadcast_to(chunk[None], out_ref.shape)


def share(parts, block_shape, devices):
    return pl.pallas_call(
        share_kernel,
        out_shape=(
            jax.ShapeDtypeStruct(block_shape, jnp.float32),
            jax.ShapeDtypeStruct((devices, CHUNK, 128), jnp.bfloat16),
        ),
        in_specs=[whole()],
        out_specs=(whole(), whole()),
        scratch_shapes=[pltpu.VMEM((HIGH, 128), jnp.float32)],
        compiler_params=vmem(8),
    )(parts)


def final_kernel(factor, n_band, parts_ref, in_ref, one_ref, two_ref, out_ref, total):
    ch = in_ref.shape[1]
    side = two_ref.shape[0]
    devices = parts_ref.shape[0]
    each = SUMS // devices
    for device in range(devices):
        tile, band = divmod(device, n_band)
        first = (band * (devices // n_band) + tile) * each
        total[first : first + each, :] = parts_ref[device].astype(jnp.float32)[0:each] * factor
    for tap in range(9):
        two_ref[tap // side, tap % side] = total[tap * ch : (tap + 1) * ch, :]
        one_ref[tap // side, tap % side] = total[(9 + tap) * ch : (10 + tap) * ch, :]
    last = total[18 * ch : 19 * ch, :]
    chans = out_ref.shape[0]
    coarse_ch = in_ref.shape[0] - chans
    flipped = last.T
    in_ref[0:coarse_ch, :] = flipped[0:coarse_ch, :]
    in_ref[coarse_ch:, :] = flipped[NOISY_AT : NOISY_AT + chans, :]
    start = OUT_AT + GRAD_AT - NOISY_AT
    out_ref[...] = flipped[start : start + chans, :]


def final(parts, n_band, width, taps, inner, chans, factor):
    f32 = jnp.float32
    return pl.pallas_call(
        functools.partial(final_kernel, factor, n_band),
        out_shape=(
            jax.ShapeDtypeStruct((inner, width), f32),
            jax.ShapeDtypeStruct(taps, f32),
            jax.ShapeDtypeStruct(taps, f32),
            jax.ShapeDtypeStruct((chans, width), f32),
        ),
        in_specs=[whole()],
        out_specs=(whole(),) * 4,
        scratch_shapes=[pltpu.VMEM((SUMS, 128), f32)],
        compiler_params=vmem(12),
    )(parts)


def halo(first, last, axis):
    count = lax.axis_size(axis)
    up = [(i, i + 1) for i in range(count - 1)]
    down = [(i + 1, i) for i in range(count - 1)]
    return lax.ppermute(last, axis, up), lax.ppermute(first, axis, down)


def ahead(parts, axis, way):
    count = lax.axis_size(axis)
    moved = [parts[0]]
    for k in range(1, count):
        pairs = [(i, (i + k * way) % count) for i in range(count)]
        moved.append(lax.ppermute(parts[k], axis, pairs))
    return moved


def per_device(
    noisy, grad_pred, coarse, margin_band, margin_slot, interp, w_in, w_conv1, w_conv2, w_out
):
    width = w_in.shape[0]
    chans, rows, cols = noisy.shape
    cells = rows * cols
    coarse_ch = coarse.shape[2]
    per_band = coarse.shape[1]
    n_band = lax.axis_size("band")
    n_tile = lax.axis_size("tile")
    local_interp = interp[0, 0]

    tile, band = lax.axis_index("tile"), lax.axis_index("band")
    flags = jnp.stack([tile > 0, tile < n_tile - 1, band > 0, band < n_band - 1])
    flags = flags.astype(jnp.float32)
    me = band.reshape(1)
    place, near, *wanted = plan(me, margin_band.reshape(-1), margin_slot, n_band)
    asked = ahead(wanted, "band", 1)
    given = make_given(noisy, grad_pred)
    asked, given, flags, late = lax.optimization_barrier((asked, given, flags, local_interp))
    stashed = pltpu.with_memory_space_constraint(stash(late), pltpu.VMEM)
    arrived = ahead(serve(asked, coarse[0]), "band", -1)
    feed, first, last, edge = make_feed(near, arrived, stashed, given)
    top, bot = halo(first, last, "tile")
    left_out, right_out, own = strips(top, bot, edge)
    left_out, *late = lax.optimization_barrier((left_out, w_in, w_out, w_conv1, w_conv2))
    weights = tuple(prep(*late))
    left, right = halo(left_out, right_out, "band")
    pred, pack = net(
        chans,
        rows,
        cols,
        n_band,
        (place, flags, feed, top, bot, left, right, own) + weights + (stashed,),
    )
    pack = lax.all_to_all(pack, "band", split_axis=0, concat_axis=0, tiled=True)
    parts = lax.all_to_all(
        merge(me, asked, pack, n_tile, coarse_ch), "tile", split_axis=0, concat_axis=0, tiled=True
    )
    coarse_grad, sums = share(
        parts, (1, per_band // n_tile) + coarse.shape[2:], n_tile * n_band
    )
    sums = lax.all_to_all(sums, ALL, split_axis=0, concat_axis=0, tiled=True)
    factor = 1.0 / math.sqrt(cells * n_tile * n_band)
    grad_in, grad_one, grad_two, grad_out = final(
        sums, n_band, width, w_conv1.shape, w_in.shape[1], chans, factor
    )
    return (pred, coarse_grad, grad_in.T, grad_one, grad_two, grad_out)


def solution(mesh):
    placed = (
        P(None, "tile", "band"),
        P(None, "tile", "band"),
        P("band", None, None, None),
        P(("tile", "band"), None),
        P(("tile", "band")),
        P("tile", "band", None, None, None),
        P(),
        P(),
        P(),
        P(),
    )
    return jax.shard_map(
        per_device,
        mesh=mesh,
        in_specs=placed,
        out_specs=(P(None, "tile", "band"), P("band", "tile", None, None), P(), P(), P(), P()),
        check_vma=False,
    )
```
